256 devices in a mesh: section: 4 (over y), tp: 4 (over x_hi, core), cp: 16 (over z, x_lo).
Axes of the slice: x: 4 (x_hi: 2, x_lo: 2; x = x_hi * 2 + x_lo), y: 4, z: 8, core: 2. Of those that a mesh axis runs over, the one named last changes fastest.
Arguments:
- query_fwd: bfloat16 [4, 2048, 8192], P('section', 'cp', 'tp')
- key_fwd: bfloat16 [4, 2048, 1024], P('section', 'cp', 'tp')
- value_forward: bfloat16 [4, 2048, 1024], P('section', 'cp', 'tp'), may hold values from -6 to 6
- segment_fwd: int32 [4, 2048], P('section', 'cp'), may hold values from 0 to 3, never falling along the last dimension, each value on 1 to 1024 neighbouring positions
- query_bwd: bfloat16 [4, 2048, 8192], P('section', 'cp', 'tp')
- key_bwd: bfloat16 [4, 2048, 1024], P('section', 'cp', 'tp')
- value_backward: bfloat16 [4, 2048, 1024], P('section', 'cp', 'tp'), may hold values from -6 to 6
- segment_bwd: int32 [4, 2048], P('section', 'cp'), may hold values from 0 to 3, never falling along the last dimension, each value on 1 to 1024 neighbouring positions
- grad_out: bfloat16 [4, 2048, 8192], P('section', 'cp', 'tp'), may hold values from -6 to 6
Outputs:
- attn_out: bfloat16 [4, 2048, 8192], P('section', 'cp', 'tp')
- grad_query: bfloat16 [4, 2048, 8192], P('section', 'cp', 'tp')
- grad_key: bfloat16 [4, 2048, 1024], P('section', 'cp', 'tp')
- grad_value: bfloat16 [4, 2048, 1024], P('section', 'cp', 'tp')
The draws below stay inside these ranges and needn't reach their ends.
Inputs may be any that keep to these rules, and one draw needn't show every extreme that they name: `segment_fwd`: document numbers never fall along a sequence. `segment_bwd`: document numbers never fall along a sequence.
All inputs are finite; a program needn't handle non-finite values.
Results may differ from the reference program's by a relative error of at most 0.013.
Values may be sent and summed in bfloat16 or wider, within the bound.
No kernel may reach another device: no remote copies, remote signals or barrier semaphores. Data moves between devices by JAX's collectives and lax.ppermute only.
A program may use at most 128 MiB of HBM per device.

```python
import math
import jax
import jax.numpy as jnp
import numpy as np
from jax import lax

QUERY_HEADS = 64
KEY_VALUE_HEADS = 8
HEAD_SIZE = 128
DOCS = 4
PACKED_LENGTH = 2048
N_SECTION = 4


def drawn_pair(key, which):
    inner = jax.random.fold_in(key, which)
    random_key_first, random_key_second = jax.random.split(inner, 2)
    group_factor = QUERY_HEADS // KEY_VALUE_HEADS
    key_rows = jax.random.truncated_normal(random_key_first, -6.0, 6.0, (N_SECTION, PACKED_LENGTH, KEY_VALUE_HEADS, HEAD_SIZE), jnp.float32)
    query_rows = jax.random.truncated_normal(random_key_second, -6.0, 6.0, (N_SECTION, PACKED_LENGTH, KEY_VALUE_HEADS, group_factor, HEAD_SIZE), jnp.float32)
    return (query_rows.reshape(N_SECTION, PACKED_LENGTH, QUERY_HEADS * HEAD_SIZE), key_rows.reshape(N_SECTION, PACKED_LENGTH, KEY_VALUE_HEADS * HEAD_SIZE))


def draw_query_fwd(key, part):
    return drawn_pair(key, 11)[0].astype(jnp.bfloat16)


def draw_key_fwd(key, part):
    return drawn_pair(key, 11)[1].astype(jnp.bfloat16)


def draw_query_bwd(key, part):
    return drawn_pair(key, 23)[0].astype(jnp.bfloat16)


def draw_key_bwd(key, part):
    return drawn_pair(key, 23)[1].astype(jnp.bfloat16)


def block_scale(key, dims, pieces, low, high):
    level, own = 1.0, jax.random.fold_in(key, 6)
    for axis_at, shards_of in pieces:
        draws = jnp.exp(jax.random.uniform(jax.random.fold_in(own, axis_at), (shards_of,), jnp.float32, low / len(pieces), high / len(pieces)))
        level = level * jnp.repeat(draws, dims[axis_at] // shards_of).reshape([-1 if axis == axis_at else 1 for axis in range(len(dims))])
    return level


def profile(amount, total, most, slope):
    portions = [(1 << 20) // math.isqrt(standing ** slope) + 1 for standing in range(2, amount + 1)]
    surplus, given = total - most - (amount - 1), [1] * (amount - 1)
    while surplus > 0:
        candidates = [i for i in range(amount - 1) if given[i] < most]
        whole, left = sum([portions[i] for i in candidates]), surplus
        for i in candidates:
            addition = min(most - given[i], max(1, left * portions[i] // whole), surplus)
            given[i] = given[i] + addition
            surplus = surplus - addition
    return np.array([most] + given)


def uneven_parts(own_key, amount, total, limit, slope):
    if amount == 2:
        one = jax.random.randint(own_key, (), max(1, total - limit), min(limit, total - 1) + 1)
        return jnp.stack([one, total - one])
    sizes = jnp.asarray(profile(amount, total, limit, slope), jnp.int32)
    twos = (amount - 1) // 2
    donor, taker = sizes[1:1 + 2 * twos:2], sizes[2:2 + 2 * twos:2]
    room = jnp.minimum(donor - 1, limit - taker)
    passed = jax.random.randint(jax.random.fold_in(own_key, 1), (twos,), 0, 1 << 20) % (room + 1)
    sizes = sizes.at[1:1 + 2 * twos:2].set(donor - passed).at[2:2 + 2 * twos:2].set(taker + passed)
    return sizes[jax.random.permutation(jax.random.fold_in(own_key, 2), amount)]


def gaussian(key, dims, scale, limit, shards=(), held_as=jnp.bfloat16):
    result = scale * jax.random.normal(key, dims, jnp.float32)
    if shards:
        result = result * block_scale(key, dims, shards, -0.22, 0.18)
    return jnp.clip(result, -limit, limit).astype(held_as)


def setup_inputs(seed: int = 0) -> dict:
    key_of = jax.random.split(jax.random.key(seed), 10)
    query_fwd = draw_query_fwd(jax.random.fold_in(key_of[9], 71), 0)
    key_fwd = draw_key_fwd(jax.random.fold_in(key_of[9], 71), 0)
    value_forward = gaussian(key_of[2], (N_SECTION, PACKED_LENGTH, KEY_VALUE_HEADS * HEAD_SIZE), 1.0, 6.0, ((0, 4), (1, 16), (2, 4)))
    segment_fwd = jax.vmap(lambda own: jnp.searchsorted(jnp.cumsum(uneven_parts(own, DOCS, PACKED_LENGTH, PACKED_LENGTH // 2, 2)), jnp.arange(PACKED_LENGTH), side="right"))(jax.random.split(key_of[3], N_SECTION)).reshape((N_SECTION, PACKED_LENGTH)).astype(jnp.int32)
    query_bwd = draw_query_bwd(jax.random.fold_in(key_of[9], 71), 0)
    key_bwd = draw_key_bwd(jax.random.fold_in(key_of[9], 71), 0)
    value_backward = gaussian(key_of[6], (N_SECTION, PACKED_LENGTH, KEY_VALUE_HEADS * HEAD_SIZE), 1.0, 6.0, ((0, 4), (1, 16), (2, 4)))
    segment_bwd = jax.vmap(lambda own: jnp.searchsorted(jnp.cumsum(uneven_parts(own, DOCS, PACKED_LENGTH, PACKED_LENGTH // 2, 2)), jnp.arange(PACKED_LENGTH), side="right"))(jax.random.split(key_of[7], N_SECTION)).reshape((N_SECTION, PACKED_LENGTH)).astype(jnp.int32)
    grad_out = gaussian(key_of[8], (N_SECTION, PACKED_LENGTH, QUERY_HEADS * HEAD_SIZE), 1.0, 6.0, ((0, 4), (1, 16), (2, 4)))
    return dict(query_fwd=query_fwd, key_fwd=key_fwd, value_forward=value_forward, segment_fwd=segment_fwd, query_bwd=query_bwd, key_bwd=key_bwd, value_backward=value_backward, segment_bwd=segment_bwd, grad_out=grad_out)


def head_stats(qf, kf, seg):
    scale = HEAD_SIZE ** -0.5
    s = jnp.einsum('iga,ja->gij', qf, kf) * scale
    pos = jnp.arange(PACKED_LENGTH)
    visible = (pos[None, :] <= pos[:, None]) & (seg[None, :] == seg[:, None])
    masked = jnp.where(visible[None], s, -jnp.inf)
    peak = jnp.max(masked, axis=-1)
    expo = jnp.where(visible[None], jnp.exp(s - peak[..., None]), 0.0)
    total = jnp.sum(expo, axis=-1)
    return s, visible, peak, expo, total


def phase_forward(query_input, key_input, value_input, seg):
    group_factor = QUERY_HEADS // KEY_VALUE_HEADS
    query_head = query_input.reshape(PACKED_LENGTH, KEY_VALUE_HEADS, group_factor, HEAD_SIZE).transpose(1, 0, 2, 3)
    key_head = key_input.reshape(PACKED_LENGTH, KEY_VALUE_HEADS, HEAD_SIZE).transpose(1, 0, 2)
    value_head = value_input.reshape(PACKED_LENGTH, KEY_VALUE_HEADS, HEAD_SIZE).transpose(1, 0, 2)

    def one_head(items):
        qx, kx, vx = items
        s, visible, peak, expo, total = head_stats(qx.astype(jnp.float32), kx.astype(jnp.float32), seg)
        p16 = expo.astype(jnp.bfloat16)
        out = jnp.einsum('gij,ja->iga', p16.astype(jnp.float32), vx.astype(jnp.float32))
        return out / total.transpose(1, 0)[..., None]

    outs = lax.map(one_head, (query_head, key_head, value_head))
    return outs.transpose(1, 0, 2, 3).reshape(PACKED_LENGTH, QUERY_HEADS * HEAD_SIZE).astype(jnp.bfloat16)


def phase_backward(query_input, key_input, value_input, seg, output_gradient):
    scale = HEAD_SIZE ** -0.5
    group_factor = QUERY_HEADS // KEY_VALUE_HEADS
    query_head = query_input.reshape(PACKED_LENGTH, KEY_VALUE_HEADS, group_factor, HEAD_SIZE).transpose(1, 0, 2, 3)
    key_head = key_input.reshape(PACKED_LENGTH, KEY_VALUE_HEADS, HEAD_SIZE).transpose(1, 0, 2)
    value_head = value_input.reshape(PACKED_LENGTH, KEY_VALUE_HEADS, HEAD_SIZE).transpose(1, 0, 2)
    head_gradient = output_gradient.reshape(PACKED_LENGTH, KEY_VALUE_HEADS, group_factor, HEAD_SIZE).transpose(1, 0, 2, 3)

    def one_head(items):
        qx, kx, vx, dx = items
        qf = qx.astype(jnp.float32)
        kf = kx.astype(jnp.float32)
        vf = vx.astype(jnp.float32)
        df = dx.astype(jnp.float32)
        s, visible, peak, expo, total = head_stats(qf, kf, seg)
        p16 = expo.astype(jnp.bfloat16)
        out = jnp.einsum('gij,ja->iga', p16.astype(jnp.float32), vf) / total.transpose(1, 0)[..., None]
        lse = peak + jnp.log(total)
        prob = jnp.where(visible[None], jnp.exp(s - lse[..., None]), 0.0)
        delta = jnp.sum(df * out, axis=-1).transpose(1, 0)
        prob16 = prob.astype(jnp.bfloat16).astype(jnp.float32)
        dvalue = jnp.einsum('gij,iga->ja', prob16, df)
        dprob = jnp.einsum('iga,ja->gij', df, vf)
        dscore = (prob * (dprob - delta[..., None])).astype(jnp.bfloat16).astype(jnp.float32)
        dquery = jnp.einsum('gij,ja->iga', dscore, kf) * scale
        dkey = jnp.einsum('gij,iga->ja', dscore, qf) * scale
        return dquery.astype(jnp.bfloat16), dkey.astype(jnp.bfloat16), dvalue.astype(jnp.bfloat16)

    dq, key_gradient, value_gradient = lax.map(one_head, (query_head, key_head, value_head, head_gradient))
    dq = dq.transpose(1, 0, 2, 3).reshape(PACKED_LENGTH, QUERY_HEADS * HEAD_SIZE)
    key_gradient = key_gradient.transpose(1, 0, 2).reshape(PACKED_LENGTH, KEY_VALUE_HEADS * HEAD_SIZE)
    value_gradient = value_gradient.transpose(1, 0, 2).reshape(PACKED_LENGTH, KEY_VALUE_HEADS * HEAD_SIZE)
    return dq, key_gradient, value_gradient


def reference(query_fwd, key_fwd, value_forward, segment_fwd, query_bwd, key_bwd, value_backward, segment_bwd, grad_out):
    outs = lax.map(lambda items: phase_forward(*items), (query_fwd, key_fwd, value_forward, segment_fwd))
    grads = lax.map(lambda items: phase_backward(*items), (query_bwd, key_bwd, value_backward, segment_bwd, grad_out))
    attn_out = jnp.roll(outs, 1, axis=0)
    grad_query = jnp.roll(grads[0], -1, axis=0)
    grad_key = jnp.roll(grads[1], -1, axis=0)
    grad_value = jnp.roll(grads[2], -1, axis=0)
    return attn_out, grad_query, grad_key, grad_value
```

```python
import math

import jax
import jax.numpy as jnp
from jax import lax
from jax.experimental import pallas as pl
from jax.experimental.pallas import tpu as pltpu
from jax.sharding import PartitionSpec as P

HEAD = 128
ROWS = 128
GROUP = 8
PAIR = 2 * ROWS
HOPS = 4
SLOTS = HOPS + 1
KEYS = SLOTS * PAIR
DOCS = 4
TAIL = 16
HALF = GROUP * HEAD
SCALE = HEAD ** (-0.5)
SCALE2 = SCALE * math.log2(math.e)
F32 = jnp.float32
BF16 = jnp.bfloat16
NT = (((1,), (1,)), ((), ()))
VMEM = pl.BlockSpec(memory_space=pltpu.VMEM)
SMEM = pl.BlockSpec(memory_space=pltpu.SMEM)


def dot(a, b):
    return jnp.dot(a, b, preferred_element_type=F32)


def dot_nt(a, b):
    return lax.dot_general(a, b, NT, preferred_element_type=F32)


def call(kernel, outs, n_in, scratch=(), flops=0, moved_bytes=2**19, name=None):
    return pl.pallas_call(
        kernel,
        out_shape=outs,
        in_specs=[SMEM] + [VMEM] * n_in,
        out_specs=[VMEM] * len(outs),
        scratch_shapes=scratch,
        compiler_params=pltpu.CompilerParams(vmem_limit_bytes=40 * 2**20),
        cost_estimate=pl.CostEstimate(flops=flops, bytes_accessed=moved_bytes, transcendentals=0),
        name=name,
    )


def shape(*dims):
    return jax.ShapeDtypeStruct(dims, BF16)


def split_kernel(where_ref, kb, vb, sb, kf, vf, sf, keep, send):
    side = where_ref[0]
    for at, part in enumerate((kb, vb, kf, vf)):
        cols = pl.ds(at * HEAD, HEAD)
        low, high = part[:, :HEAD], part[:, HEAD:]
        keep[:ROWS, cols] = jnp.where(side == 0, low, high)
        send[:ROWS, cols] = jnp.where(side == 0, high, low)
    for out in (keep, send):
        out[ROWS:, :] = jnp.zeros((TAIL, 4 * HEAD), BF16)
        for at, seg in ((0, sb), (2, sf)):
            row = seg[...].astype(F32).astype(BF16)
            out[ROWS:, at * HEAD : (at + 1) * HEAD] = jnp.broadcast_to(row, (TAIL, ROWS))


def join_kernel(where_ref, keep, got, eb, ef):
    del where_ref
    for at, out in ((0, eb), (2, ef)):
        cols = slice(at * HEAD, (at + 2) * HEAD)
        out[:ROWS, :] = keep[:ROWS, cols]
        out[ROWS:PAIR, :] = got[:ROWS, cols]
        out[PAIR:, :ROWS] = keep[ROWS:, at * HEAD : (at + 1) * HEAD]
        out[PAIR:, ROWS:] = got[ROWS:, at * HEAD : (at + 1) * HEAD]


def other_half_kernel(where_ref, *refs):
    side = where_ref[0]
    start = pl.multiple_of((1 - side) * HALF, HALF)
    out = refs[-1]
    for at, ref in enumerate(refs[:-1]):
        out[:, at * HALF : (at + 1) * HALF] = ref[:, pl.ds(start, HALF)]


def whole_kernel(where_ref, own, cross, out):
    side = where_ref[0]
    out[:, pl.ds(pl.multiple_of(side * HALF, HALF), HALF)] = own[...]
    out[:, pl.ds(pl.multiple_of((1 - side) * HALF, HALF), HALF)] = cross[...]


def fill_cap(where_ref, blocks, cap):
    side, depth = where_ref[0], where_ref[1]
    segs = [b[PAIR : PAIR + 1, :].astype(F32) for b in blocks]
    start = jnp.zeros((1, PAIR), F32)
    for d in range(DOCS):
        first = jnp.sum((segs[0] < d).astype(F32), axis=1, keepdims=True)
        for k in range(1, SLOTS):
            same = jnp.sum((segs[k] == d).astype(F32), axis=1, keepdims=True)
            first = first - jnp.where(depth >= k, same, 0.0)
        start = jnp.where(segs[0] == d, first, start)
    start = start.astype(jnp.int32)
    lane = lax.broadcasted_iota(jnp.int32, (ROWS, PAIR), 1)
    row = jnp.where(lane < ROWS, lane + side * ROWS, lane - side * ROWS)
    for k in range(SLOTS):
        for part in range(2):
            block = side if part == 0 else 1 - side
            key = lax.broadcasted_iota(jnp.int32, (ROWS, PAIR), 0) + (block * ROWS - k * PAIR)
            seen = (key >= start) & (key <= row)
            cap[pl.ds(k * PAIR + part * ROWS, ROWS), :] = jnp.where(seen, 3.0e38, -jnp.inf)


def fill_window(blocks, kwin, vwin):
    for k, b in enumerate(blocks):
        kwin[pl.ds(k * PAIR, PAIR), :] = b[:PAIR, :HEAD]
        vwin[pl.ds(k * PAIR, PAIR), :] = b[:PAIR, HEAD:]


def head_rows(side, own, other, g, base):
    cols = pl.ds(pl.multiple_of(side * HALF + g * HEAD, HEAD), HEAD)
    return jnp.concatenate([own[:, cols], other[:, pl.ds(base + g * HEAD, HEAD)]], axis=0)


def fwd_kernel(where_ref, q_ref, qx_ref, *refs):
    blocks, (own_ref, cross_ref, kwin, vwin, cap, s_ref) = refs[:SLOTS], refs[SLOTS:]
    side = where_ref[0]
    fill_window(blocks, kwin, vwin)
    fill_cap(where_ref, blocks, cap)
    vt = vwin[...].T
    for g in range(GROUP):
        queries = head_rows(side, q_ref, qx_ref, g, 0)
        masked = jnp.minimum(dot_nt(kwin[...], queries), cap[...])
        s_ref[...] = masked
        peak = jnp.max(masked, axis=0, keepdims=True)
        expo = jnp.exp2((s_ref[...] - peak) * SCALE2)
        total = jnp.sum(expo, axis=0, keepdims=True)
        out = (dot(vt, expo.astype(BF16)) / total).T.astype(BF16)
        cols = slice(g * HEAD, (g + 1) * HEAD)
        own_ref[:, cols] = out[:ROWS]
        cross_ref[:, cols] = out[ROWS:]


def bwd_kernel(where_ref, q_ref, d_ref, qdx_ref, *refs):
    blocks = refs[:SLOTS]
    own_ref, cross_ref = refs[SLOTS : SLOTS + 2]
    parts = refs[SLOTS + 2 : 2 * SLOTS + 2]
    kwin, vwin, cap, s_ref, dp_ref, p_ref, ds_ref, qs_ref, gs_ref = refs[2 * SLOTS + 2 :]
    side = where_ref[0]
    fill_window(blocks, kwin, vwin)
    fill_cap(where_ref, blocks, cap)
    kt = kwin[...].T
    for g in range(GROUP):
        cols = pl.ds(g * PAIR, PAIR)
        queries = head_rows(side, q_ref, qdx_ref, g, 0)
        grads = head_rows(side, d_ref, qdx_ref, g, HALF)
        qs_ref[cols, :] = queries
        gs_ref[cols, :] = grads
        masked = jnp.minimum(dot_nt(kwin[...], queries), cap[...])
        s_ref[...] = masked
        peak = jnp.max(masked, axis=0, keepdims=True)
        dp = dot_nt(vwin[...], grads)
        expo = jnp.exp2((s_ref[...] - peak) * SCALE2)
        s_ref[...] = expo
        dp_ref[...] = dp
        inv = 1.0 / jnp.sum(expo, axis=0, keepdims=True)
        delta = jnp.sum(expo * dp, axis=0, keepdims=True) * inv
        prob = s_ref[...] * inv
        p_ref[:, cols] = prob.astype(BF16)
        ds = (prob * (dp_ref[...] - delta)).astype(BF16)
        ds_ref[:, cols] = ds
        dq = (dot(kt, ds) * SCALE).T.astype(BF16)
        at = slice(g * HEAD, (g + 1) * HEAD)
        own_ref[:, at] = dq[:ROWS]
        cross_ref[:, at] = dq[ROWS:]
    for k in range(SLOTS):
        rows = pl.ds(k * PAIR, PAIR)
        parts[k][:, :HEAD] = (dot(ds_ref[rows, :], qs_ref[...]) * SCALE).astype(BF16)
        parts[k][:, HEAD:] = dot(p_ref[rows, :], gs_ref[...]).astype(BF16)


def window_scratch():
    return [
        pltpu.VMEM((KEYS, HEAD), BF16),
        pltpu.VMEM((KEYS, HEAD), BF16),
        pltpu.VMEM((KEYS, PAIR), F32),
        pltpu.VMEM((KEYS, PAIR), F32),
    ]


MATMUL = 2 * GROUP * PAIR * KEYS * HEAD


def run_fwd(where, query, crossed, blocks):
    halves = [shape(ROWS, HALF)] * 2
    return call(fwd_kernel, halves, 2 + SLOTS, window_scratch(), 2 * MATMUL, 2**21, "fwd")(
        where, query, crossed, *blocks
    )


def run_bwd(where, query, grad, crossed, blocks):
    outs = [shape(ROWS, HALF)] * 2 + [shape(PAIR, 2 * HEAD)] * SLOTS
    scratch = window_scratch() + [
        pltpu.VMEM((KEYS, PAIR), F32),
        pltpu.VMEM((KEYS, GROUP * PAIR), BF16),
        pltpu.VMEM((KEYS, GROUP * PAIR), BF16),
        pltpu.VMEM((GROUP * PAIR, HEAD), BF16),
        pltpu.VMEM((GROUP * PAIR, HEAD), BF16),
    ]
    out = call(bwd_kernel, outs, 3 + SLOTS, scratch, 5 * MATMUL, 2**22, "bwd")(
        where, query, grad, crossed, *blocks
    )
    return out[0], out[1], out[2:]


def along_z(block, distance):
    n = lax.axis_size("cp")
    return lax.ppermute(block, "cp", [(i, (i + 2 * distance) % n) for i in range(n)])


def swapped(block):
    return lax.ppermute(block, "cp", [(i, i ^ 1) for i in range(lax.axis_size("cp"))])


def handed(block, distance):
    n = lax.axis_size("section")
    return lax.ppermute(block, "section", [(i, (i + distance) % n) for i in range(n)])


def handed_across(block, distance):
    n, m = lax.axis_size("section"), lax.axis_size("cp")
    route = [
        (s * m + c, (s + distance) % n * m + (c ^ 1)) for s in range(n) for c in range(m)
    ]
    return lax.ppermute(block, ("section", "cp"), route)


def chain(block):
    blocks = [block]
    for _ in range(HOPS):
        blocks.append(along_z(blocks[-1], 1))
    return blocks


def per_device(qf, kf, vf, sf, qb, kb, vb, sb, grad):
    index = lax.axis_index("cp")
    side = index % 2
    where = jnp.stack([side, index // 2]).astype(jnp.int32)
    qf, kf, vf, qb, kb, vb, grad = (a[0] for a in (qf, kf, vf, qb, kb, vb, grad))
    keep, send = call(split_kernel, [shape(ROWS + TAIL, 4 * HEAD)] * 2, 6, name="split")(
        where, kb, vb, sb, kf, vf, sf
    )
    got = swapped(send)
    eb, ef = call(join_kernel, [shape(PAIR + TAIL, 2 * HEAD)] * 2, 2, name="join")(
        where, keep, got
    )
    blocks_b = chain(eb)
    (send_b,) = call(other_half_kernel, [shape(ROWS, 2 * HALF)], 2, name="half_b")(where, qb, grad)
    crossed_b = swapped(send_b)
    blocks_f = chain(ef)
    (send_f,) = call(other_half_kernel, [shape(ROWS, HALF)], 1, name="half_f")(where, qf)
    crossed_f = swapped(send_f)

    dq_own, dq_cross, parts = run_bwd(where, qb, grad, crossed_b, blocks_b)
    whole = [shape(ROWS, 2 * HALF)]
    (grad_query,) = call(whole_kernel, whole, 2, name="whole_dq")(
        where, handed(dq_own, -1), handed_across(dq_cross, -1)
    )
    o_own, o_cross = run_fwd(where, qf, crossed_f, blocks_f)
    (attn_out,) = call(whole_kernel, whole, 2, name="whole_o")(
        where, handed(o_own, 1), handed_across(o_cross, 1)
    )
    running = parts[HOPS]
    for k in range(HOPS - 1, -1, -1):
        total = parts[k].astype(F32) + along_z(running, -1).astype(F32)
        running = total.astype(BF16)
    mine = handed(running[:ROWS], -1)
    theirs = handed_across(running[ROWS:], -1)
    low = jnp.where(side == 0, mine, theirs)
    high = jnp.where(side == 0, theirs, mine)
    grad_key = jnp.concatenate([low[:, :HEAD], high[:, :HEAD]], axis=1)
    grad_value = jnp.concatenate([low[:, HEAD:], high[:, HEAD:]], axis=1)
    return attn_out[None], grad_query[None], grad_key[None], grad_value[None]


def solution(mesh):
    wide = P("section", "cp", "tp")
    flat = P("section", "cp")
    return jax.shard_map(
        per_device,
        mesh=mesh,
        in_specs=(wide, wide, wide, flat, wide, wide, wide, flat, wide),
        out_specs=(wide, wide, wide, wide),
        check_vma=False,
    )
```

```python
import functools
import math

import jax
import jax.numpy as jnp
from jax import lax
from jax.experimental import pallas as pl
from jax.experimental.pallas import tpu as pltpu
from jax.sharding import PartitionSpec as P

HEAD = 128
ROWS = 128
GROUP = 8
PAIR = 2 * ROWS
SLOTS = 5
KEYS = SLOTS * PAIR
DOCS = 4
TAIL = 16
HALF = GROUP * HEAD
SCALE = HEAD ** (-0.5)
SCALE2 = SCALE * math.log2(math.e)
F32 = jnp.float32
BF16 = jnp.bfloat16
NT = (((1,), (1,)), ((), ()))
VMEM = pl.BlockSpec(memory_space=pltpu.VMEM)
SMEM = pl.BlockSpec(memory_space=pltpu.SMEM)
ANY = pl.BlockSpec(memory_space=pl.ANY)
HBM = pl.BlockSpec(memory_space=pltpu.HBM)


def dot(a, b):
    return jnp.dot(a, b, preferred_element_type=F32)


def dot_nt(a, b):
    return lax.dot_general(a, b, NT, preferred_element_type=F32)


def call(kernel, outs, ins, scratch=(), flops=0, moved_bytes=2**19, name=None, place=VMEM, limit=4):
    return pl.pallas_call(
        kernel,
        out_shape=outs,
        in_specs=[SMEM] + ([VMEM] * ins if isinstance(ins, int) else ins),
        out_specs=[place] * len(outs),
        scratch_shapes=scratch,
        compiler_params=pltpu.CompilerParams(vmem_limit_bytes=limit * 2**20),
        cost_estimate=pl.CostEstimate(flops=flops, bytes_accessed=moved_bytes, transcendentals=0),
        name=name,
    )


def shape(*dims):
    return jax.ShapeDtypeStruct(dims, BF16)


def fetched(copies, sems):
    started = [pltpu.make_async_copy(a, b, sems.at[i]) for i, (a, b) in enumerate(copies)]
    for c in started:
        c.start()
    for c in started:
        c.wait()


def split_kernel(where_ref, *refs):
    side = where_ref[0]
    ins, (keep, send, keys, segs, sems) = refs[:6], refs[6:]
    copies = []
    for i in range(2):
        copies += [(ins[3 * i], keys.at[2 * i]), (ins[3 * i + 1], keys.at[2 * i + 1])]
        copies.append((ins[3 * i + 2], segs.at[i]))
    fetched(copies, sems)
    for at in range(4):
        cols = slice(at * HEAD, (at + 1) * HEAD)
        low, high = keys[at, :, :HEAD], keys[at, :, HEAD:]
        keep[:ROWS, cols] = jnp.where(side == 0, low, high)
        send[:ROWS, cols] = jnp.where(side == 0, high, low)
        row = jnp.broadcast_to(segs[at // 2].astype(F32).astype(BF16), (TAIL, ROWS))
        for out in (keep, send):
            out[ROWS:, cols] = row


def join_kernel(where_ref, keep, got, half_in, eb, ef, half_out):
    del where_ref, half_in, half_out
    for at, out in ((0, eb), (2, ef)):
        cols = slice(at * HEAD, (at + 2) * HEAD)
        one = slice(at * HEAD, (at + 1) * HEAD)
        out[:ROWS, :] = keep[:ROWS, cols]
        out[ROWS:PAIR, :] = got[:ROWS, cols]
        out[PAIR:, :HEAD] = keep[ROWS:, one]
        out[PAIR:, HEAD:] = got[ROWS:, one]


def other_half_kernel(where_ref, *refs, count):
    start = pl.multiple_of((1 - where_ref[0]) * HALF, HALF)
    ins, out, sems = refs[:count], refs[-2], refs[-1]
    fetched(
        [
            (ref.at[:, pl.ds(start, HALF)], out.at[:, at * HALF : (at + 1) * HALF])
            for at, ref in enumerate(ins)
        ],
        sems,
    )


def total_kernel(where_ref, *refs):
    del where_ref
    own, cross = refs[-2:]
    for i, out in enumerate((own, cross)):
        rows = pl.ds(i * ROWS, ROWS)
        out[...] = sum(r[rows, :].astype(F32) for r in refs[:SLOTS]).astype(BF16)


def final_kernel(where_ref, *refs):
    side = where_ref[0]
    ins, (o, dq, dk, dv), sems = refs[:6], refs[6:10], refs[10]
    copies = []
    for i, at in enumerate((side, 1 - side)):
        wide = pl.ds(pl.multiple_of(at * HALF, HALF), HALF)
        head = pl.ds(pl.multiple_of(at * HEAD, HEAD), HEAD)
        copies.append((ins[i], o.at[:, wide]))
        copies.append((ins[2 + i], dq.at[:, wide]))
        copies.append((ins[4 + i].at[:, :HEAD], dk.at[:, head]))
        copies.append((ins[4 + i].at[:, HEAD:], dv.at[:, head]))
    fetched(copies, sems)


def fill_cap(where_ref, blocks, cap):
    side, depth = where_ref[0], where_ref[1]
    segs = [b[PAIR : PAIR + 1, :].astype(F32) for b in blocks]
    start = jnp.zeros((1, PAIR), F32)
    for d in range(DOCS):
        first = jnp.sum((segs[0] < d).astype(F32), axis=1, keepdims=True)
        for k in range(1, SLOTS):
            same = jnp.sum((segs[k] == d).astype(F32), axis=1, keepdims=True)
            first = first - jnp.where(depth >= k, same, 0.0)
        start = jnp.where(segs[0] == d, first, start)
    start = start.astype(jnp.int32)
    lane = lax.broadcasted_iota(jnp.int32, (ROWS, PAIR), 1)
    row = jnp.where(lane < ROWS, lane + side * ROWS, lane - side * ROWS)
    for k in range(SLOTS):
        for part in range(2):
            block = side if part == 0 else 1 - side
            key = lax.broadcasted_iota(jnp.int32, (ROWS, PAIR), 0) + (block * ROWS - k * PAIR)
            seen = (key >= start) & (key <= row)
            cap[pl.ds(k * PAIR + part * ROWS, ROWS), :] = jnp.where(seen, 3.0e38, -jnp.inf)


def slot(k):
    return slice(k * PAIR, (k + 1) * PAIR)


def folded(x, reduce):
    return reduce(x.reshape(PAIR // 8, 8, PAIR), axis=0)


def joined(running, new, op):
    return new if running is None else op(running, new)


def score_slot(k, lanes, keys, turned, cap, s_ref):
    masked = jnp.minimum(dot(keys, turned), cap[slot(k), :])
    s_ref[slot(k), lanes] = masked
    return folded(masked, jnp.max)


def exponentials(k, lanes, s_ref, peak):
    return jnp.exp2((s_ref[slot(k), lanes] - peak) * SCALE2)


def head_rows(own, crossed, g, offset=0):
    at = slice(g * HEAD, (g + 1) * HEAD)
    far = slice(offset + g * HEAD, offset + (g + 1) * HEAD)
    return jnp.concatenate([own[:, at], crossed[:, far]], axis=0)


def put_rows(g, columns, own, crossed):
    rows = columns.T.astype(BF16)
    at = slice(g * HEAD, (g + 1) * HEAD)
    own[:, at] = rows[:ROWS]
    crossed[:, at] = rows[ROWS:]


ALL = slice(0, PAIR)


def fwd_kernel(where_ref, q_hbm, qx_ref, *refs):
    blocks, refs = refs[:SLOTS], refs[SLOTS + 1 :]
    o_own, o_cross, cap, s_ref, e_ref, vt_ref, q_ref, turned, sems = refs
    base = pl.multiple_of(where_ref[0] * HALF, HALF)
    fetch = pltpu.make_async_copy(q_hbm.at[:, pl.ds(base, HALF)], q_ref, sems.at[0])
    fetch.start()
    fill_cap(where_ref, blocks, cap)
    for k, b in enumerate(blocks):
        vt_ref[:, slot(k)] = b[:PAIR, HEAD:].T
    fetch.wait()

    def turn(g):
        turned[g % 2] = head_rows(q_ref, qx_ref, g).T

    peak = None
    turn(0)
    for k in range(SLOTS):
        peak = joined(peak, score_slot(k, ALL, blocks[k][:PAIR, :HEAD], turned[0], cap, s_ref.at[0]), jnp.maximum)
    for g in range(GROUP):
        now, later = g % 2, (g + 1) % 2
        top = jnp.max(peak, axis=0, keepdims=True)
        peak = total = None
        if g + 1 < GROUP:
            turn(g + 1)
        for k in range(SLOTS):
            expo = exponentials(k, ALL, s_ref.at[now], top)
            e_ref[now, slot(k), :] = expo.astype(BF16)
            total = joined(total, folded(expo, jnp.sum), jnp.add)
            if g + 1 < GROUP:
                new = score_slot(k, ALL, blocks[k][:PAIR, :HEAD], turned[later], cap, s_ref.at[later])
                peak = joined(peak, new, jnp.maximum)
        inv = 1.0 / jnp.sum(total, axis=0, keepdims=True)
        put_rows(g, dot(vt_ref[...], e_ref[now]) * inv, o_own, o_cross)


def bwd_kernel(where_ref, q_hbm, d_hbm, qdx_ref, *refs):
    blocks, refs = refs[:SLOTS], refs[SLOTS:]
    dq_own, dq_cross = refs[:2]
    parts, refs = refs[2 : SLOTS + 2], refs[SLOTS + 2 :]
    cap, s_ref, dp_ref, e_ref, ds_ref, qs_ref, gs_ref, acc, kt_ref, qd_ref, turned, sems = refs
    base = pl.multiple_of(where_ref[0] * HALF, HALF)
    fetch = [
        pltpu.make_async_copy(h.at[:, pl.ds(base, HALF)], qd_ref.at[i], sems.at[i])
        for i, h in enumerate((q_hbm, d_hbm))
    ]
    for c in fetch:
        c.start()
    fill_cap(where_ref, blocks, cap)
    for k, b in enumerate(blocks):
        kt_ref[:, slot(k)] = b[:PAIR, :HEAD].T
    for c in fetch:
        c.wait()

    def span_of(g):
        return slice(g * PAIR, (g + 1) * PAIR)

    def key_terms(k, span, last):
        dk = dot(ds_ref[slot(k), span], qs_ref[span, :])
        dv = dot(e_ref[slot(k), span], gs_ref[span, :])
        if last:
            parts[k][:, :HEAD] = ((dk + acc[0, slot(k), :]) * SCALE).astype(BF16)
            parts[k][:, HEAD:] = (dv + acc[1, slot(k), :]).astype(BF16)
        else:
            acc[0, slot(k), :] = dk
            acc[1, slot(k), :] = dv

    def query_terms(g, inv):
        put_rows(g, dot(kt_ref[...], ds_ref[:, span_of(g)]) * (inv * SCALE), dq_own, dq_cross)

    half = GROUP // 2
    first, second = slice(0, half * PAIR), slice(half * PAIR, GROUP * PAIR)

    def turn(g):
        turned[g % 2, 0] = head_rows(qd_ref.at[0], qdx_ref, g).T
        turned[g % 2, 1] = head_rows(qd_ref.at[1], qdx_ref, g, HALF).T

    peak = None
    turn(0)
    for k in range(SLOTS):
        peak = joined(peak, score_slot(k, ALL, blocks[k][:PAIR, :HEAD], turned[0, 0], cap, s_ref.at[0]), jnp.maximum)
    for g in range(GROUP):
        now, later = g % 2, (g + 1) % 2
        cols = span_of(g)
        top = jnp.max(peak, axis=0, keepdims=True)
        peak = total = inner = None
        for k in range(SLOTS):
            expo = exponentials(k, ALL, s_ref.at[now], top)
            dp = dot(blocks[k][:PAIR, HEAD:], turned[now, 1])
            e_ref[slot(k), cols] = expo.astype(BF16)
            dp_ref[now, slot(k), :] = dp
            total = joined(total, folded(expo, jnp.sum), jnp.add)
            inner = joined(inner, folded(expo * dp, jnp.sum), jnp.add)
            if k == 0 and g > 0:
                query_terms(g - 1, inv)
        inv = 1.0 / jnp.sum(total, axis=0, keepdims=True)
        delta = jnp.sum(inner, axis=0, keepdims=True) * inv
        factor = jnp.broadcast_to(inv, (HEAD, PAIR)).T
        qs_ref[cols, :] = (head_rows(qd_ref.at[0], qdx_ref, g).astype(F32) * factor).astype(BF16)
        gs_ref[cols, :] = (head_rows(qd_ref.at[1], qdx_ref, g, HALF).astype(F32) * factor).astype(BF16)
        if g + 1 < GROUP:
            turn(g + 1)
        for k in range(SLOTS):
            ds = (dp_ref[now, slot(k), :] - delta).astype(BF16)
            ds_ref[slot(k), cols] = e_ref[slot(k), cols] * ds
            if g + 1 < GROUP:
                new = score_slot(k, ALL, blocks[k][:PAIR, :HEAD], turned[later, 0], cap, s_ref.at[later])
                peak = joined(peak, new, jnp.maximum)
        if g >= half:
            for k in (2 * (g - half), 2 * (g - half) + 1):
                if k < SLOTS:
                    key_terms(k, first, False)
    query_terms(GROUP - 1, inv)
    for k in range(SLOTS):
        key_terms(k, second, True)


MATMUL = 2 * GROUP * PAIR * KEYS * HEAD


def run_fwd(where, query, crossed, blocks, after):
    scratch = [
        pltpu.VMEM((KEYS, PAIR), F32),
        pltpu.VMEM((2, KEYS, PAIR), F32),
        pltpu.VMEM((2, KEYS, PAIR), BF16),
        pltpu.VMEM((HEAD, KEYS), BF16),
        pltpu.VMEM((ROWS, HALF), BF16),
        pltpu.VMEM((2, HEAD, PAIR), BF16),
        pltpu.SemaphoreType.DMA((1,)),
    ]
    return call(
        fwd_kernel,
        [shape(ROWS, HALF)] * 2,
        [HBM] + [VMEM] * (1 + SLOTS) + [ANY] * 1,
        scratch,
        2 * MATMUL,
        2**21,
        "fwd",
        limit=20,
    )(where, query, crossed, *blocks, *after)


def run_bwd(where, query, grad, crossed, blocks):
    outs = [shape(ROWS, HALF)] * 2 + [shape(PAIR, 2 * HEAD)] * SLOTS
    scratch = [
        pltpu.VMEM((KEYS, PAIR), F32),
        pltpu.VMEM((2, KEYS, PAIR), F32),
        pltpu.VMEM((2, KEYS, PAIR), F32),
        pltpu.VMEM((KEYS, GROUP * PAIR), BF16),
        pltpu.VMEM((KEYS, GROUP * PAIR), BF16),
        pltpu.VMEM((GROUP * PAIR, HEAD), BF16),
        pltpu.VMEM((GROUP * PAIR, HEAD), BF16),
        pltpu.VMEM((2, KEYS, HEAD), F32),
        pltpu.VMEM((HEAD, KEYS), BF16),
        pltpu.VMEM((2, ROWS, HALF), BF16),
        pltpu.VMEM((2, 2, HEAD, PAIR), BF16),
        pltpu.SemaphoreType.DMA((2,)),
    ]
    out = call(
        bwd_kernel,
        outs,
        [HBM] * 2 + [VMEM] * (1 + SLOTS),
        scratch,
        5 * MATMUL,
        2**22,
        "bwd",
        limit=32,
    )(where, query, grad, crossed, *blocks)
    return out[0], out[1], out[2:]


def along_z(block, distance):
    n = lax.axis_size("cp")
    return lax.ppermute(block, "cp", [(i, (i + 2 * distance) % n) for i in range(n)])


def swapped(block):
    return lax.ppermute(block, "cp", [(i, i ^ 1) for i in range(lax.axis_size("cp"))])


def handed(block, distance):
    n = lax.axis_size("section")
    return lax.ppermute(block, "section", [(i, (i + distance) % n) for i in range(n)])


def handed_across(block, distance):
    n, m = lax.axis_size("section"), lax.axis_size("cp")
    route = [
        (s * m + c, (s + distance) % n * m + (c ^ 1)) for s in range(n) for c in range(m)
    ]
    return lax.ppermute(block, ("section", "cp"), route)


def split(where, *arrays):
    scratch = [
        pltpu.VMEM((4, ROWS, 2 * HEAD), BF16),
        pltpu.VMEM((2, 1, ROWS), jnp.int32),
        pltpu.SemaphoreType.DMA((6,)),
    ]
    outs = [shape(ROWS + TAIL, 4 * HEAD)] * 2
    return call(split_kernel, outs, [HBM] * 6, scratch, name="split")(where, *arrays)


def join(where, keep, got, through):
    return pl.pallas_call(
        join_kernel,
        out_shape=[shape(PAIR + TAIL, 2 * HEAD)] * 2 + [shape(*through.shape)],
        in_specs=[SMEM] + [VMEM] * 2 + [ANY],
        out_specs=[VMEM] * 2 + [ANY],
        input_output_aliases={3: 2},
        compiler_params=pltpu.CompilerParams(vmem_limit_bytes=4 * 2**20),
        name="join",
    )(where, keep, got, through)


def tied_kernel(where_ref, held, after, out):
    del where_ref, held, after, out


def tied(where, held, after):
    return pl.pallas_call(
        tied_kernel,
        out_shape=shape(*held.shape),
        in_specs=[SMEM, ANY, ANY],
        out_specs=ANY,
        input_output_aliases={1: 0},
        compiler_params=pltpu.CompilerParams(vmem_limit_bytes=2**20),
        name="tied",
    )(where, held, after)


def other_half(where, arrays, after, name):
    (out,) = call(
        functools.partial(other_half_kernel, count=len(arrays)),
        [shape(ROWS, len(arrays) * HALF)],
        [HBM] * len(arrays) + [ANY],
        [pltpu.SemaphoreType.DMA((len(arrays),))],
        name=name,
    )(where, *arrays, after)
    return out


def per_device(qf, kf, vf, sf, qb, kb, vb, sb, grad):
    index = lax.axis_index("cp")
    side = index % 2
    where = jnp.stack([side, index // 2]).astype(jnp.int32)
    qf, kf, vf, qb, kb, vb, grad = (a[0] for a in (qf, kf, vf, qb, kb, vb, grad))
    qf, kf, vf, sf, qb, kb, vb, sb, grad = (
        pltpu.with_memory_space_constraint(a, pltpu.HBM)
        for a in (qf, kf, vf, sf, qb, kb, vb, sb, grad)
    )

    keep, send = split(where, kb, vb, sb, kf, vf, sf)
    half_b = other_half(where, (qb, grad), send, "half_b")
    b0, f0, half_b = join(where, keep, swapped(send), half_b)
    b4 = along_z(b0, -2)
    b2 = along_z(b0, 2)
    b1 = along_z(b0, 1)
    crossed_b = swapped(half_b)
    b4 = along_z(b4, -2)
    b3 = along_z(b2, 1)
    half_f = other_half(where, (qf,), b2, "half_f")
    f0 = tied(where, f0, b2)
    blocks_f = [f0] + [along_z(f0, k) for k in (1, 2, 3, 4)]
    crossed_f = swapped(half_f)

    dq_own, dq_cross, parts = run_bwd(where, qb, grad, crossed_b, (b0, b1, b2, b3, b4))
    terms = [parts[0]] + [along_z(parts[k], -k) for k in (1, 2, 3, 4)]
    o_own, o_cross = run_fwd(where, qf, crossed_f, blocks_f, (terms[1],))
    dq = handed(dq_own, -1), handed_across(dq_cross, -1)
    own, cross = call(
        total_kernel, [shape(ROWS, 2 * HEAD)] * 2, SLOTS, name="total"
    )(where, *terms)
    outs = call(
        final_kernel,
        [shape(ROWS, 2 * HALF)] * 2 + [shape(ROWS, 2 * HEAD)] * 2,
        6,
        [pltpu.SemaphoreType.DMA((8,))],
        name="final",
        place=HBM,
    )(
        where,
        handed(o_own, 1),
        handed_across(o_cross, 1),
        *dq,
        handed(own, -1),
        handed_across(cross, -1),
    )
    return tuple(out[None] for out in outs)


def solution(mesh):
    wide = P("section", "cp", "tp")
    flat = P("section", "cp")
    return jax.shard_map(
        per_device,
        mesh=mesh,
        in_specs=(wide, wide, wide, flat, wide, wide, wide, flat, wide),
        out_specs=(wide, wide, wide, wide),
        check_vma=False,
    )
```

```python
import functools
import math

import jax
import jax.numpy as jnp
from jax import lax
from jax.experimental import pallas as pl
from jax.experimental.pallas import tpu as pltpu
from jax.sharding import PartitionSpec as P

HEAD = 128
ROWS = 128
GROUP = 8
PAIR = 2 * ROWS
SLOTS = 5
KEYS = SLOTS * PAIR
DOCS = 4
TAIL = 16
HALF = GROUP * HEAD
SCALE = HEAD ** (-0.5)
SCALE2 = SCALE * math.log2(math.e)
F32 = jnp.float32
BF16 = jnp.bfloat16
NT = (((1,), (1,)), ((), ()))
VMEM = pl.BlockSpec(memory_space=pltpu.VMEM)
SMEM = pl.BlockSpec(memory_space=pltpu.SMEM)
ANY = pl.BlockSpec(memory_space=pl.ANY)
HBM = pl.BlockSpec(memory_space=pltpu.HBM)


def dot(a, b):
    return jnp.dot(a, b, preferred_element_type=F32)


def dot_nt(a, b):
    return lax.dot_general(a, b, NT, preferred_element_type=F32)


def call(kernel, outs, ins, scratch=(), flops=0, moved_bytes=2**19, name=None, place=VMEM, limit=4):
    return pl.pallas_call(
        kernel,
        out_shape=outs,
        in_specs=[SMEM] + ([VMEM] * ins if isinstance(ins, int) else ins),
        out_specs=place if isinstance(place, list) else [place] * len(outs),
        scratch_shapes=scratch,
        compiler_params=pltpu.CompilerParams(vmem_limit_bytes=limit * 2**20),
        cost_estimate=pl.CostEstimate(flops=flops, bytes_accessed=moved_bytes, transcendentals=0),
        name=name,
    )


def shape(*dims):
    return jax.ShapeDtypeStruct(dims, BF16)


def fetched(copies, sems):
    started = [pltpu.make_async_copy(a, b, sems.at[i]) for i, (a, b) in enumerate(copies)]
    for c in started:
        c.start()
    for c in started:
        c.wait()


def split_kernel(where_ref, *refs):
    side = where_ref[0]
    ins, (keep, send, keys, segs, sems) = refs[:6], refs[6:]
    copies = []
    for i in range(2):
        copies += [(ins[3 * i], keys.at[2 * i]), (ins[3 * i + 1], keys.at[2 * i + 1])]
        copies.append((ins[3 * i + 2], segs.at[i]))
    fetched(copies, sems)
    for at in range(4):
        cols = slice(at * HEAD, (at + 1) * HEAD)
        low, high = keys[at, :, :HEAD], keys[at, :, HEAD:]
        keep[:ROWS, cols] = jnp.where(side == 0, low, high)
        send[:ROWS, cols] = jnp.where(side == 0, high, low)
        row = jnp.broadcast_to(segs[at // 2].astype(F32).astype(BF16), (TAIL, ROWS))
        for out in (keep, send):
            out[ROWS:, cols] = row


def join_kernel(where_ref, keep, got, half_in, eb, ef, half_out):
    del where_ref, half_in, half_out
    for at, out in ((0, eb), (2, ef)):
        cols = slice(at * HEAD, (at + 2) * HEAD)
        one = slice(at * HEAD, (at + 1) * HEAD)
        out[:ROWS, :] = keep[:ROWS, cols]
        out[ROWS:PAIR, :] = got[:ROWS, cols]
        out[PAIR:, :HEAD] = keep[ROWS:, one]
        out[PAIR:, HEAD:] = got[ROWS:, one]


def other_half_kernel(where_ref, *refs, count):
    start = pl.multiple_of((1 - where_ref[0]) * HALF, HALF)
    ins, out, sems = refs[:count], refs[-2], refs[-1]
    fetched(
        [
            (ref.at[:, pl.ds(start, HALF)], out.at[:, at * HALF : (at + 1) * HALF])
            for at, ref in enumerate(ins)
        ],
        sems,
    )


def total_kernel(where_ref, *refs):
    del where_ref
    refs[-1][...] = sum(r[...].astype(F32) for r in refs[:SLOTS]).astype(BF16)


def output_kernel(where_ref, own, cross, o, token, sems):
    side = where_ref[0]
    token[...] = jnp.zeros_like(token)
    fetched(
        [
            (part, o.at[:, pl.ds(pl.multiple_of(at * HALF, HALF), HALF)])
            for part, at in ((own, side), (cross, 1 - side))
        ],
        sems,
    )


def final_kernel(where_ref, *refs):
    side = where_ref[0]
    ins, (dq, dk, dv), sems = refs[:4], refs[5:8], refs[8]
    copies = []
    for i, at in enumerate((side, 1 - side)):
        wide = pl.ds(pl.multiple_of(at * HALF, HALF), HALF)
        head = pl.ds(pl.multiple_of(at * HEAD, HEAD), HEAD)
        rows = pl.ds(i * ROWS, ROWS)
        copies.append((ins[i], dq.at[:, wide]))
        copies.append((ins[2 + i].at[rows, :HEAD], dk.at[:, head]))
        copies.append((ins[2 + i].at[rows, HEAD:], dv.at[:, head]))
    fetched(copies, sems)


def fill_cap(where_ref, blocks, cap):
    side, depth = where_ref[0], where_ref[1]
    segs = [b[PAIR : PAIR + 1, :].astype(F32) for b in blocks]
    start = jnp.zeros((1, PAIR), F32)
    for d in range(DOCS):
        first = jnp.sum((segs[0] < d).astype(F32), axis=1, keepdims=True)
        for k in range(1, SLOTS):
            same = jnp.sum((segs[k] == d).astype(F32), axis=1, keepdims=True)
            first = first - jnp.where(depth >= k, same, 0.0)
        start = jnp.where(segs[0] == d, first, start)
    start = start.astype(jnp.int32)
    lane = lax.broadcasted_iota(jnp.int32, (ROWS, PAIR), 1)
    row = jnp.where(lane < ROWS, lane + side * ROWS, lane - side * ROWS)
    for k in range(SLOTS):
        for part in range(2):
            block = side if part == 0 else 1 - side
            key = lax.broadcasted_iota(jnp.int32, (ROWS, PAIR), 0) + (block * ROWS - k * PAIR)
            seen = (key >= start) & (key <= row)
            cap[pl.ds(k * PAIR + part * ROWS, ROWS), :] = jnp.where(seen, 3.0e38, -jnp.inf)


def slot(k):
    return slice(k * PAIR, (k + 1) * PAIR)


def folded(x, reduce):
    return reduce(x.reshape(PAIR // 8, 8, PAIR), axis=0)


def joined(running, new, op):
    return new if running is None else op(running, new)


def bounded(k, s_ref, cap):
    return jnp.minimum(s_ref[slot(k), :], cap[slot(k), :])


def row_peak(s_ref, cap):
    peak = None
    for k in range(SLOTS):
        peak = joined(peak, folded(bounded(k, s_ref, cap), jnp.max), jnp.maximum)
    return jnp.max(peak, axis=0, keepdims=True)


def exponentials(k, s_ref, cap, peak):
    return jnp.exp2((bounded(k, s_ref, cap) - peak) * SCALE2)


def head_rows(own, crossed, g, offset=0):
    at = slice(g * HEAD, (g + 1) * HEAD)
    far = slice(offset + g * HEAD, offset + (g + 1) * HEAD)
    return jnp.concatenate([own[:, at], crossed[:, far]], axis=0)


def put_rows(g, columns, own, crossed):
    rows = columns.T.astype(BF16)
    at = slice(g * HEAD, (g + 1) * HEAD)
    own[:, at] = rows[:ROWS]
    crossed[:, at] = rows[ROWS:]


def fwd_kernel(where_ref, q_hbm, qx_ref, *refs):
    blocks, refs = refs[:SLOTS], refs[SLOTS + 1 :]
    o_own, o_cross, cap, s_ref, e_ref, keys, vt_ref, q_ref, sems = refs
    base = pl.multiple_of(where_ref[0] * HALF, HALF)
    fetch = pltpu.make_async_copy(q_hbm.at[:, pl.ds(base, HALF)], q_ref, sems.at[0])
    fetch.start()
    fill_cap(where_ref, blocks, cap)
    for k, b in enumerate(blocks):
        keys[slot(k), :] = b[:PAIR, :HEAD]
        vt_ref[:, slot(k)] = b[:PAIR, HEAD:].T
    fetch.wait()

    def score(g):
        s_ref[g % 2] = dot(keys[...], head_rows(q_ref, qx_ref, g, 2 * HALF).T)

    score(0)
    for g in range(GROUP):
        now = g % 2
        if g + 1 < GROUP:
            score(g + 1)
        top = row_peak(s_ref.at[now], cap)
        total = None
        for k in range(SLOTS):
            expo = exponentials(k, s_ref.at[now], cap, top)
            e_ref[now, slot(k), :] = expo.astype(BF16)
            total = joined(total, folded(expo, jnp.sum), jnp.add)
        inv = 1.0 / jnp.sum(total, axis=0, keepdims=True)
        put_rows(g, dot(vt_ref[...], e_ref[now]) * inv, o_own, o_cross)


def bwd_kernel(where_ref, q_hbm, d_hbm, qdx_ref, *refs):
    blocks, refs = refs[:SLOTS], refs[SLOTS:]
    dq_own, dq_cross = refs[:2]
    parts, refs = refs[2 : SLOTS + 2], refs[SLOTS + 2 :]
    cap, s_ref, dp_ref, e_ref, ds_ref, qs_ref, gs_ref, acc, keys, values, kt_ref, qd_ref, sems = refs
    base = pl.multiple_of(where_ref[0] * HALF, HALF)
    fetch = [
        pltpu.make_async_copy(h.at[:, pl.ds(base, HALF)], qd_ref.at[i], sems.at[i])
        for i, h in enumerate((q_hbm, d_hbm))
    ]
    for c in fetch:
        c.start()
    fill_cap(where_ref, blocks, cap)
    for k, b in enumerate(blocks):
        keys[slot(k), :] = b[:PAIR, :HEAD]
        values[slot(k), :] = b[:PAIR, HEAD:]
        kt_ref[:, slot(k)] = b[:PAIR, :HEAD].T
    for c in fetch:
        c.wait()

    def rows_of(which, g):
        return head_rows(qd_ref.at[which], qdx_ref, g, which * HALF)

    def products(g):
        s_ref[g % 2] = dot(keys[...], rows_of(0, g).T)
        dp_ref[g % 2] = dot(values[...], rows_of(1, g).T)

    def span_of(g, count=1):
        return slice(g * PAIR, (g + count) * PAIR)

    def key_terms(g):
        span = span_of(g, 2)
        both = dot(ds_ref[:, span], qs_ref[span, :]), dot(e_ref[:, span], gs_ref[span, :])
        for i, terms in enumerate(both):
            acc[i] = terms if g == 0 else acc[i] + terms

    products(0)
    for g in range(GROUP):
        now = g % 2
        cols = span_of(g)
        if g + 1 < GROUP:
            products(g + 1)
        if g > 1 and g % 2 == 0:
            key_terms(g - 2)
        top = row_peak(s_ref.at[now], cap)
        total = inner = None
        for k in range(SLOTS):
            expo = exponentials(k, s_ref.at[now], cap, top)
            e_ref[slot(k), cols] = expo.astype(BF16)
            total = joined(total, folded(expo, jnp.sum), jnp.add)
            inner = joined(inner, folded(expo * dp_ref[now, slot(k), :], jnp.sum), jnp.add)
        inv = 1.0 / jnp.sum(total, axis=0, keepdims=True)
        delta = jnp.sum(inner, axis=0, keepdims=True) * inv
        factor = jnp.broadcast_to(inv, (HEAD, PAIR)).T
        qs_ref[cols, :] = (rows_of(0, g).astype(F32) * factor).astype(BF16)
        gs_ref[cols, :] = (rows_of(1, g).astype(F32) * factor).astype(BF16)
        for k in range(SLOTS):
            ds = (dp_ref[now, slot(k), :] - delta).astype(BF16)
            ds_ref[slot(k), cols] = e_ref[slot(k), cols] * ds
        put_rows(g, dot(kt_ref[...], ds_ref[:, cols]) * (inv * SCALE), dq_own, dq_cross)
    key_terms(GROUP - 2)
    for k in range(SLOTS):
        parts[k][:, :HEAD] = (acc[0, slot(k), :] * SCALE).astype(BF16)
        parts[k][:, HEAD:] = acc[1, slot(k), :].astype(BF16)


MATMUL = 2 * GROUP * PAIR * KEYS * HEAD
FINAL_FLOPS = 2 * MATMUL


def run_fwd(where, query, crossed, blocks, after):
    scratch = [
        pltpu.VMEM((KEYS, PAIR), F32),
        pltpu.VMEM((2, KEYS, PAIR), F32),
        pltpu.VMEM((2, KEYS, PAIR), BF16),
        pltpu.VMEM((KEYS, HEAD), BF16),
        pltpu.VMEM((HEAD, KEYS), BF16),
        pltpu.VMEM((ROWS, HALF), BF16),
        pltpu.SemaphoreType.DMA((1,)),
    ]
    return call(
        fwd_kernel,
        [shape(ROWS, HALF)] * 2,
        [HBM] + [VMEM] * (1 + SLOTS) + [ANY] * 1,
        scratch,
        2 * MATMUL,
        2**21,
        "fwd",
        limit=20,
    )(where, query, crossed, *blocks, *after)


def run_bwd(where, query, grad, crossed, blocks):
    outs = [shape(ROWS, HALF)] * 2 + [shape(PAIR, 2 * HEAD)] * SLOTS
    scratch = [
        pltpu.VMEM((KEYS, PAIR), F32),
        pltpu.VMEM((2, KEYS, PAIR), F32),
        pltpu.VMEM((2, KEYS, PAIR), F32),
        pltpu.VMEM((KEYS, GROUP * PAIR), BF16),
        pltpu.VMEM((KEYS, GROUP * PAIR), BF16),
        pltpu.VMEM((GROUP * PAIR, HEAD), BF16),
        pltpu.VMEM((GROUP * PAIR, HEAD), BF16),
        pltpu.VMEM((2, KEYS, HEAD), F32),
        pltpu.VMEM((KEYS, HEAD), BF16),
        pltpu.VMEM((KEYS, HEAD), BF16),
        pltpu.VMEM((HEAD, KEYS), BF16),
        pltpu.VMEM((2, ROWS, HALF), BF16),
        pltpu.SemaphoreType.DMA((2,)),
    ]
    out = call(
        bwd_kernel,
        outs,
        [HBM] * 2 + [VMEM] * (1 + SLOTS),
        scratch,
        5 * MATMUL,
        2**22,
        "bwd",
        limit=32,
    )(where, query, grad, crossed, *blocks)
    return out[0], out[1], out[2:]


def along_z(block, distance):
    n = lax.axis_size("cp")
    return lax.ppermute(block, "cp", [(i, (i + 2 * distance) % n) for i in range(n)])


def swapped(block):
    return lax.ppermute(block, "cp", [(i, i ^ 1) for i in range(lax.axis_size("cp"))])


def handed(block, distance):
    n = lax.axis_size("section")
    return lax.ppermute(block, "section", [(i, (i + distance) % n) for i in range(n)])


def handed_across(block, distance):
    n, m = lax.axis_size("section"), lax.axis_size("cp")
    route = [
        (s * m + c, (s + distance) % n * m + (c ^ 1)) for s in range(n) for c in range(m)
    ]
    return lax.ppermute(block, ("section", "cp"), route)


def split(where, *arrays):
    scratch = [
        pltpu.VMEM((4, ROWS, 2 * HEAD), BF16),
        pltpu.VMEM((2, 1, ROWS), jnp.int32),
        pltpu.SemaphoreType.DMA((6,)),
    ]
    outs = [shape(ROWS + TAIL, 4 * HEAD)] * 2
    return call(split_kernel, outs, [HBM] * 6, scratch, name="split")(where, *arrays)


def join(where, keep, got, through):
    return pl.pallas_call(
        join_kernel,
        out_shape=[shape(PAIR + TAIL, 2 * HEAD)] * 2 + [shape(*through.shape)],
        in_specs=[SMEM] + [VMEM] * 2 + [ANY],
        out_specs=[VMEM] * 2 + [ANY],
        input_output_aliases={3: 2},
        compiler_params=pltpu.CompilerParams(vmem_limit_bytes=4 * 2**20),
        name="join",
    )(where, keep, got, through)


def tied_kernel(where_ref, held, after, out):
    del where_ref, held, after, out


def tied(where, held, after):
    return pl.pallas_call(
        tied_kernel,
        out_shape=shape(*held.shape),
        in_specs=[SMEM, ANY, ANY],
        out_specs=ANY,
        input_output_aliases={1: 0},
        compiler_params=pltpu.CompilerParams(vmem_limit_bytes=2**20),
        name="tied",
    )(where, held, after)


def other_half(where, arrays, after, name):
    (out,) = call(
        functools.partial(other_half_kernel, count=len(arrays)),
        [shape(ROWS, len(arrays) * HALF)],
        [HBM] * len(arrays) + [ANY],
        [pltpu.SemaphoreType.DMA((len(arrays),))],
        name=name,
    )(where, *arrays, after)
    return out


def per_device(qf, kf, vf, sf, qb, kb, vb, sb, grad):
    index = lax.axis_index("cp")
    side = index % 2
    where = jnp.stack([side, index // 2]).astype(jnp.int32)
    qf, kf, vf, qb, kb, vb, grad = (a[0] for a in (qf, kf, vf, qb, kb, vb, grad))
    qf, kf, vf, sf, qb, kb, vb, sb, grad = (
        pltpu.with_memory_space_constraint(a, pltpu.HBM)
        for a in (qf, kf, vf, sf, qb, kb, vb, sb, grad)
    )

    keep, send = split(where, kb, vb, sb, kf, vf, sf)
    halves = other_half(where, (qb, grad, qf), send, "halves")
    b0, f0, halves = join(where, keep, swapped(send), halves)
    b4 = along_z(b0, -2)
    b2 = along_z(b0, 2)
    b1 = along_z(b0, 1)
    crossed = swapped(halves)
    b4 = along_z(b4, -2)
    b3 = along_z(b2, 1)
    f0 = tied(where, f0, b2)
    blocks_f = [f0] + [along_z(f0, k) for k in (1, 2, 3, 4)]

    dq_own, dq_cross, parts = run_bwd(where, qb, grad, crossed, (b0, b1, b2, b3, b4))
    terms = [parts[0]] + [along_z(parts[k], -k) for k in range(1, SLOTS)]
    dq = handed(dq_own, -1), handed_across(dq_cross, -1)
    o_own, o_cross = run_fwd(where, qf, crossed, blocks_f, (terms[1],))
    dq = handed(dq_own, -1), handed_across(dq_cross, -1)
    (summed,) = call(
        total_kernel, [shape(PAIR, 2 * HEAD)], [VMEM] * SLOTS + [ANY] * 2, name="total"
    )(where, *terms, *dq)
    received = handed(summed, -1)
    attn_out, token = call(
        output_kernel,
        [shape(ROWS, 2 * HALF), shape(TAIL, HEAD)],
        2,
        [pltpu.SemaphoreType.DMA((2,))],
        FINAL_FLOPS,
        name="output",
        place=[HBM, VMEM],
    )(where, handed(o_own, 1), handed_across(o_cross, 1))
    grads = call(
        final_kernel,
        [shape(ROWS, 2 * HALF)] + [shape(ROWS, 2 * HEAD)] * 2,
        [VMEM] * 4 + [ANY],
        [pltpu.SemaphoreType.DMA((6,))],
        name="final",
        place=HBM,
    )(where, *dq, received, swapped(received), token)
    return tuple(out[None] for out in (attn_out, *grads))


def solution(mesh):
    wide = P("section", "cp", "tp")
    flat = P("section", "cp")
    return jax.shard_map(
        per_device,
        mesh=mesh,
        in_specs=(wide, wide, wide, flat, wide, wide, wide, flat, wide),
        out_specs=(wide, wide, wide, wide),
        check_vma=False,
    )
```

```python
import functools
import math

import jax
import jax.numpy as jnp
from jax import lax
from jax.experimental import pallas as pl
from jax.experimental.pallas import tpu as pltpu
from jax.sharding import PartitionSpec as P

HEAD = 128
ROWS = 128
GROUP = 8
PAIR = 2 * ROWS
SLOTS = 5
KEYS = SLOTS * PAIR
DOCS = 4
TAIL = 16
HALF = GROUP * HEAD
SCALE = HEAD ** (-0.5)
SCALE2 = SCALE * math.log2(math.e)
F32 = jnp.float32
BF16 = jnp.bfloat16
NT = (((1,), (1,)), ((), ()))
VMEM = pl.BlockSpec(memory_space=pltpu.VMEM)
SMEM = pl.BlockSpec(memory_space=pltpu.SMEM)
ANY = pl.BlockSpec(memory_space=pl.ANY)
HBM = pl.BlockSpec(memory_space=pltpu.HBM)


def dot(a, b):
    return jnp.dot(a, b, preferred_element_type=F32)


def dot_nt(a, b):
    return lax.dot_general(a, b, NT, preferred_element_type=F32)


def call(kernel, outs, ins, scratch=(), flops=0, moved_bytes=2**19, name=None, place=VMEM, limit=4):
    return pl.pallas_call(
        kernel,
        out_shape=outs,
        in_specs=[SMEM] + ([VMEM] * ins if isinstance(ins, int) else ins),
        out_specs=place if isinstance(place, list) else [place] * len(outs),
        scratch_shapes=scratch,
        compiler_params=pltpu.CompilerParams(vmem_limit_bytes=limit * 2**20),
        cost_estimate=pl.CostEstimate(flops=flops, bytes_accessed=moved_bytes, transcendentals=0),
        name=name,
    )


def shape(*dims):
    return jax.ShapeDtypeStruct(dims, BF16)


def fetched(copies, sems):
    started = [pltpu.make_async_copy(a, b, sems.at[i]) for i, (a, b) in enumerate(copies)]
    for c in started:
        c.start()
    for c in started:
        c.wait()


def split_kernel(where_ref, *refs):
    side = where_ref[0]
    ins, (keep, send, keys, segs, sems) = refs[:6], refs[6:]
    copies = []
    for i in range(2):
        copies += [(ins[3 * i], keys.at[2 * i]), (ins[3 * i + 1], keys.at[2 * i + 1])]
        copies.append((ins[3 * i + 2], segs.at[i]))
    fetched(copies, sems)
    for at in range(4):
        cols = slice(at * HEAD, (at + 1) * HEAD)
        low, high = keys[at, :, :HEAD], keys[at, :, HEAD:]
        keep[:ROWS, cols] = jnp.where(side == 0, low, high)
        send[:ROWS, cols] = jnp.where(side == 0, high, low)
        row = jnp.broadcast_to(segs[at // 2].astype(F32).astype(BF16), (TAIL, ROWS))
        for out in (keep, send):
            out[ROWS:, cols] = row


def join_kernel(where_ref, keep, got, half_in, eb, ef, half_out):
    del where_ref, half_in, half_out
    for at, out in ((0, eb), (2, ef)):
        cols = slice(at * HEAD, (at + 2) * HEAD)
        one = slice(at * HEAD, (at + 1) * HEAD)
        out[:ROWS, :] = keep[:ROWS, cols]
        out[ROWS:PAIR, :] = got[:ROWS, cols]
        out[PAIR:, :HEAD] = keep[ROWS:, one]
        out[PAIR:, HEAD:] = got[ROWS:, one]


def halves_kernel(where_ref, *refs):
    ins, (mine, theirs, sems) = refs[:3], refs[4:]
    copies = []
    for i, ref in enumerate(ins):
        cols = slice(i * HALF, (i + 1) * HALF)
        for side, out in ((where_ref[0], mine), (1 - where_ref[0], theirs)):
            start = pl.multiple_of(side * HALF, HALF)
            copies.append((ref.at[:, pl.ds(start, HALF)], out.at[:, cols]))
    fetched(copies, sems)


def total_kernel(where_ref, *refs):
    del where_ref
    refs[-1][...] = sum(r[...].astype(F32) for r in refs[:SLOTS]).astype(BF16)


def output_kernel(where_ref, own, cross, o, token, sems):
    side = where_ref[0]
    token[...] = jnp.zeros_like(token)
    fetched(
        [
            (part, o.at[:, pl.ds(pl.multiple_of(at * HALF, HALF), HALF)])
            for part, at in ((own, side), (cross, 1 - side))
        ],
        sems,
    )


def final_kernel(where_ref, *refs):
    side = where_ref[0]
    ins, (dq, dk, dv), sems = refs[:4], refs[5:8], refs[8]
    copies = []
    for i, at in enumerate((side, 1 - side)):
        wide = pl.ds(pl.multiple_of(at * HALF, HALF), HALF)
        head = pl.ds(pl.multiple_of(at * HEAD, HEAD), HEAD)
        copies.append((ins[i], dq.at[:, wide]))
        copies.append((ins[2 + i].at[:ROWS, :HEAD], dk.at[:, head]))
        copies.append((ins[2 + i].at[:ROWS, HEAD:], dv.at[:, head]))
    fetched(copies, sems)


def fill_cap(where_ref, blocks, cap):
    side, depth = where_ref[0], where_ref[1]
    segs = [b[PAIR : PAIR + 1, :].astype(F32) for b in blocks]
    start = jnp.zeros((1, PAIR), F32)
    for d in range(DOCS):
        first = jnp.sum((segs[0] < d).astype(F32), axis=1, keepdims=True)
        for k in range(1, SLOTS):
            same = jnp.sum((segs[k] == d).astype(F32), axis=1, keepdims=True)
            first = first - jnp.where(depth >= k, same, 0.0)
        start = jnp.where(segs[0] == d, first, start)
    start = start.astype(jnp.int32)
    lane = lax.broadcasted_iota(jnp.int32, (ROWS, PAIR), 1)
    row = jnp.where(lane < ROWS, lane + side * ROWS, lane - side * ROWS)
    for k in range(SLOTS):
        for part in range(2):
            block = side if part == 0 else 1 - side
            key = lax.broadcasted_iota(jnp.int32, (ROWS, PAIR), 0) + (block * ROWS - k * PAIR)
            seen = (key >= start) & (key <= row)
            cap[pl.ds(k * PAIR + part * ROWS, ROWS), :] = jnp.where(seen, 3.0e38, -jnp.inf)


def slot(k):
    return slice(k * PAIR, (k + 1) * PAIR)


def folded(x, reduce):
    return reduce(x.reshape(PAIR // 8, 8, PAIR), axis=0)


def joined(running, new, op):
    return new if running is None else op(running, new)


def bounded(k, s_ref, cap):
    return jnp.minimum(s_ref[slot(k), :], cap[slot(k), :])


def row_peak(s_ref, cap):
    peak = None
    for k in range(SLOTS):
        peak = joined(peak, folded(bounded(k, s_ref, cap), jnp.max), jnp.maximum)
    return jnp.max(peak, axis=0, keepdims=True)


def exponentials(k, s_ref, cap, peak):
    return jnp.exp2((bounded(k, s_ref, cap) - peak) * SCALE2)


def head_rows(own, crossed, g, offset=0):
    at = slice(offset + g * HEAD, offset + (g + 1) * HEAD)
    return jnp.concatenate([own[:, at], crossed[:, at]], axis=0)


def put_rows(g, columns, own, crossed):
    rows = columns.T.astype(BF16)
    at = slice(g * HEAD, (g + 1) * HEAD)
    own[:, at] = rows[:ROWS]
    crossed[:, at] = rows[ROWS:]


def fwd_kernel(where_ref, q_ref, qx_ref, *refs):
    blocks, refs = refs[:SLOTS], refs[SLOTS + 1 :]
    o_own, o_cross, cap, s_ref, e_ref, keys, vt_ref = refs
    fill_cap(where_ref, blocks, cap)
    for k, b in enumerate(blocks):
        keys[slot(k), :] = b[:PAIR, :HEAD]
        vt_ref[:, slot(k)] = b[:PAIR, HEAD:].T

    def score(g):
        s_ref[g % 2] = dot(keys[...], head_rows(q_ref, qx_ref, g, 2 * HALF).T)

    score(0)
    for g in range(GROUP):
        now = g % 2
        if g + 1 < GROUP:
            score(g + 1)
        top = row_peak(s_ref.at[now], cap)
        total = None
        for k in range(SLOTS):
            expo = exponentials(k, s_ref.at[now], cap, top)
            e_ref[now, slot(k), :] = expo.astype(BF16)
            total = joined(total, folded(expo, jnp.sum), jnp.add)
        inv = 1.0 / jnp.sum(total, axis=0, keepdims=True)
        put_rows(g, dot(vt_ref[...], e_ref[now]) * inv, o_own, o_cross)


def bwd_kernel(where_ref, qd_ref, qdx_ref, *refs):
    blocks, refs = refs[:SLOTS], refs[SLOTS:]
    dq_own, dq_cross = refs[:2]
    parts, refs = refs[2 : SLOTS + 2], refs[SLOTS + 2 :]
    cap, s_ref, dp_ref, e_ref, ds_ref, qs_ref, gs_ref, acc, keys, values, kt_ref, turned = refs
    fill_cap(where_ref, blocks, cap)
    for k, b in enumerate(blocks):
        keys[slot(k), :] = b[:PAIR, :HEAD]
        values[slot(k), :] = b[:PAIR, HEAD:]
        kt_ref[:, slot(k)] = b[:PAIR, :HEAD].T

    def rows_of(which, g):
        return head_rows(qd_ref, qdx_ref, g, which * HALF)

    def products(g):
        for i, (block, out) in enumerate(((keys, s_ref), (values, dp_ref))):
            turned[g % 2, i] = rows_of(i, g).T
            out[g % 2] = dot(block[...], turned[g % 2, i])

    def span_of(g, count=1):
        return slice(g * PAIR, (g + count) * PAIR)

    def key_terms(g):
        span = span_of(g, 2)
        both = dot_nt(qs_ref[:, span], ds_ref[:, span]), dot_nt(gs_ref[:, span], e_ref[:, span])
        for i, terms in enumerate(both):
            acc[i] = terms if g == 0 else acc[i] + terms

    products(0)
    for g in range(GROUP):
        now = g % 2
        cols = span_of(g)
        if g + 1 < GROUP:
            products(g + 1)
        if g > 1 and g % 2 == 0:
            key_terms(g - 2)
        top = row_peak(s_ref.at[now], cap)
        total = inner = None
        for k in range(SLOTS):
            expo = exponentials(k, s_ref.at[now], cap, top)
            e_ref[slot(k), cols] = expo.astype(BF16)
            total = joined(total, folded(expo, jnp.sum), jnp.add)
            inner = joined(inner, folded(expo * dp_ref[now, slot(k), :], jnp.sum), jnp.add)
        inv = 1.0 / jnp.sum(total, axis=0, keepdims=True)
        delta = jnp.sum(inner, axis=0, keepdims=True) * inv
        qs_ref[:, cols] = (turned[now, 0].astype(F32) * inv).astype(BF16)
        gs_ref[:, cols] = (turned[now, 1].astype(F32) * inv).astype(BF16)
        for k in range(SLOTS):
            ds = (dp_ref[now, slot(k), :] - delta).astype(BF16)
            ds_ref[slot(k), cols] = e_ref[slot(k), cols] * ds
        put_rows(g, dot(kt_ref[...], ds_ref[:, cols]) * (inv * SCALE), dq_own, dq_cross)
    key_terms(GROUP - 2)
    for k in range(SLOTS):
        parts[k][:, :HEAD] = (acc[0, :, slot(k)] * SCALE).T.astype(BF16)
        parts[k][:, HEAD:] = acc[1, :, slot(k)].T.astype(BF16)


MATMUL = 2 * GROUP * PAIR * KEYS * HEAD
FINAL_FLOPS = 2 * MATMUL


def run_fwd(where, own, crossed, blocks, after):
    scratch = [
        pltpu.VMEM((KEYS, PAIR), F32),
        pltpu.VMEM((2, KEYS, PAIR), F32),
        pltpu.VMEM((2, KEYS, PAIR), BF16),
        pltpu.VMEM((KEYS, HEAD), BF16),
        pltpu.VMEM((HEAD, KEYS), BF16),
    ]
    return call(
        fwd_kernel,
        [shape(ROWS, HALF)] * 2,
        [VMEM] * (2 + SLOTS) + [ANY] * 1,
        scratch,
        2 * MATMUL,
        2**21,
        "fwd",
        limit=20,
    )(where, own, crossed, *blocks, *after)


def run_bwd(where, own, crossed, blocks):
    outs = [shape(ROWS, HALF)] * 2 + [shape(PAIR, 2 * HEAD)] * SLOTS
    scratch = [
        pltpu.VMEM((KEYS, PAIR), F32),
        pltpu.VMEM((2, KEYS, PAIR), F32),
        pltpu.VMEM((2, KEYS, PAIR), F32),
        pltpu.VMEM((KEYS, GROUP * PAIR), BF16),
        pltpu.VMEM((KEYS, GROUP * PAIR), BF16),
        pltpu.VMEM((HEAD, GROUP * PAIR), BF16),
        pltpu.VMEM((HEAD, GROUP * PAIR), BF16),
        pltpu.VMEM((2, HEAD, KEYS), F32),
        pltpu.VMEM((KEYS, HEAD), BF16),
        pltpu.VMEM((KEYS, HEAD), BF16),
        pltpu.VMEM((HEAD, KEYS), BF16),
        pltpu.VMEM((2, 2, HEAD, PAIR), BF16),
    ]
    out = call(
        bwd_kernel,
        outs,
        2 + SLOTS,
        scratch,
        5 * MATMUL,
        2**22,
        "bwd",
        limit=32,
    )(where, own, crossed, *blocks)
    return out[0], out[1], out[2:]


def along_z(block, distance):
    n = lax.axis_size("cp")
    return lax.ppermute(block, "cp", [(i, (i + 2 * distance) % n) for i in range(n)])


def swapped(block):
    return lax.ppermute(block, "cp", [(i, i ^ 1) for i in range(lax.axis_size("cp"))])


def handed(block, distance):
    n = lax.axis_size("section")
    return lax.ppermute(block, "section", [(i, (i + distance) % n) for i in range(n)])


def handed_across(block, distance):
    n, m = lax.axis_size("section"), lax.axis_size("cp")
    route = [
        (s * m + c, (s + distance) % n * m + (c ^ 1)) for s in range(n) for c in range(m)
    ]
    return lax.ppermute(block, ("section", "cp"), route)


def split(where, *arrays):
    scratch = [
        pltpu.VMEM((4, ROWS, 2 * HEAD), BF16),
        pltpu.VMEM((2, 1, ROWS), jnp.int32),
        pltpu.SemaphoreType.DMA((6,)),
    ]
    outs = [shape(ROWS + TAIL, 4 * HEAD)] * 2
    return call(split_kernel, outs, [HBM] * 6, scratch, name="split")(where, *arrays)


def join(where, keep, got, through):
    return pl.pallas_call(
        join_kernel,
        out_shape=[shape(PAIR + TAIL, 2 * HEAD)] * 2 + [shape(*through.shape)],
        in_specs=[SMEM] + [VMEM] * 2 + [ANY],
        out_specs=[VMEM] * 2 + [ANY],
        input_output_aliases={3: 2},
        compiler_params=pltpu.CompilerParams(vmem_limit_bytes=4 * 2**20),
        name="join",
    )(where, keep, got, through)


def tied_kernel(where_ref, held, after, out):
    del where_ref, held, after, out


def tied(where, held, after):
    return pl.pallas_call(
        tied_kernel,
        out_shape=shape(*held.shape),
        in_specs=[SMEM, ANY, ANY],
        out_specs=ANY,
        input_output_aliases={1: 0},
        compiler_params=pltpu.CompilerParams(vmem_limit_bytes=2**20),
        name="tied",
    )(where, held, after)


def per_device(qf, kf, vf, sf, qb, kb, vb, sb, grad):
    index = lax.axis_index("cp")
    side = index % 2
    where = jnp.stack([side, index // 2]).astype(jnp.int32)
    qf, kf, vf, qb, kb, vb, grad = (a[0] for a in (qf, kf, vf, qb, kb, vb, grad))
    qf, kf, vf, sf, qb, kb, vb, sb, grad = (
        pltpu.with_memory_space_constraint(a, pltpu.HBM)
        for a in (qf, kf, vf, sf, qb, kb, vb, sb, grad)
    )

    keep, send = split(where, kb, vb, sb, kf, vf, sf)
    own, halves = call(
        halves_kernel,
        [shape(ROWS, 3 * HALF)] * 2,
        [HBM] * 3 + [ANY],
        [pltpu.SemaphoreType.DMA((6,))],
        name="halves",
    )(where, qb, grad, qf, send)
    b0, f0, halves = join(where, keep, swapped(send), halves)
    b4 = along_z(b0, -2)
    b2 = along_z(b0, 2)
    b1 = along_z(b0, 1)
    crossed = swapped(halves)
    b4 = along_z(b4, -2)
    b3 = along_z(b2, 1)
    f0 = tied(where, f0, b2)
    blocks_f = [f0] + [along_z(f0, k) for k in (1, 2, 3, 4)]

    dq_own, dq_cross, parts = run_bwd(where, own, crossed, (b0, b1, b2, b3, b4))
    terms = [parts[0]] + [along_z(parts[k], -k) for k in range(1, SLOTS)]
    dq = handed(dq_own, -1), handed_across(dq_cross, -1)
    o_own, o_cross = run_fwd(where, own, crossed, blocks_f, (terms[1],))
    dq = handed(dq_own, -1), handed_across(dq_cross, -1)
    (summed,) = call(
        total_kernel, [shape(PAIR, 2 * HEAD)], [VMEM] * SLOTS + [ANY] * 2, name="total"
    )(where, *terms, *dq)
    received = handed(summed, -1)
    attn_out, token = call(
        output_kernel,
        [shape(ROWS, 2 * HALF), shape(TAIL, HEAD)],
        2,
        [pltpu.SemaphoreType.DMA((2,))],
        FINAL_FLOPS,
        name="output",
        place=[HBM, VMEM],
    )(where, handed(o_own, 1), handed_across(o_cross, 1))
    grads = call(
        final_kernel,
        [shape(ROWS, 2 * HALF)] + [shape(ROWS, 2 * HEAD)] * 2,
        [VMEM] * 4 + [ANY],
        [pltpu.SemaphoreType.DMA((6,))],
        name="final",
        place=HBM,
    )(where, *dq, received, swapped(received[ROWS:]), token)
    return tuple(out[None] for out in (attn_out, *grads))


def solution(mesh):
    wide = P("section", "cp", "tp")
    flat = P("section", "cp")
    return jax.shard_map(
        per_device,
        mesh=mesh,
        in_specs=(wide, wide, wide, flat, wide, wide, wide, flat, wide),
        out_specs=(wide, wide, wide, wide),
        check_vma=False,
    )
```

```python
import functools
import math

import jax
import jax.numpy as jnp
from jax import lax
from jax.experimental import pallas as pl
from jax.experimental.pallas import tpu as pltpu
from jax.sharding import PartitionSpec as P

HEAD = 128
ROWS = 128
GROUP = 8
PAIR = 2 * ROWS
SLOTS = 5
KEYS = SLOTS * PAIR
DOCS = 4
TAIL = 16
HALF = GROUP * HEAD
SCALE = HEAD ** (-0.5)
SCALE2 = SCALE * math.log2(math.e)
F32 = jnp.float32
BF16 = jnp.bfloat16
NT = (((1,), (1,)), ((), ()))
VMEM = pl.BlockSpec(memory_space=pltpu.VMEM)
SMEM = pl.BlockSpec(memory_space=pltpu.SMEM)
ANY = pl.BlockSpec(memory_space=pl.ANY)
HBM = pl.BlockSpec(memory_space=pltpu.HBM)


def dot(a, b):
    return jnp.dot(a, b, preferred_element_type=F32)


def dot_nt(a, b):
    return lax.dot_general(a, b, NT, preferred_element_type=F32)


def call(kernel, outs, ins, scratch=(), flops=0, moved_bytes=2**19, name=None, place=VMEM, limit=4):
    return pl.pallas_call(
        kernel,
        out_shape=outs,
        in_specs=[SMEM] + ([VMEM] * ins if isinstance(ins, int) else ins),
        out_specs=place if isinstance(place, list) else [place] * len(outs),
        scratch_shapes=scratch,
        compiler_params=pltpu.CompilerParams(vmem_limit_bytes=limit * 2**20),
        cost_estimate=pl.CostEstimate(flops=flops, bytes_accessed=moved_bytes, transcendentals=0),
        name=name,
    )


def shape(*dims):
    return jax.ShapeDtypeStruct(dims, BF16)


def fetched(copies, sems):
    started = [pltpu.make_async_copy(a, b, sems.at[i]) for i, (a, b) in enumerate(copies)]
    for c in started:
        c.start()
    for c in started:
        c.wait()


def split_kernel(where_ref, *refs):
    side = where_ref[0]
    ins, (keep, send, keys, segs, sems) = refs[:6], refs[6:]
    copies = []
    for i in range(2):
        copies += [(ins[3 * i], keys.at[2 * i]), (ins[3 * i + 1], keys.at[2 * i + 1])]
        copies.append((ins[3 * i + 2], segs.at[i]))
    fetched(copies, sems)
    for at in range(4):
        cols = slice(at * HEAD, (at + 1) * HEAD)
        low, high = keys[at, :, :HEAD], keys[at, :, HEAD:]
        keep[:ROWS, cols] = jnp.where(side == 0, low, high)
        send[:ROWS, cols] = jnp.where(side == 0, high, low)
        row = jnp.broadcast_to(segs[at // 2].astype(F32).astype(BF16), (TAIL, ROWS))
        for out in (keep, send):
            out[ROWS:, cols] = row


def join_kernel(where_ref, keep, got, half_in, eb, ef, half_out):
    del where_ref, half_in, half_out
    for at, out in ((0, eb), (2, ef)):
        cols = slice(at * HEAD, (at + 2) * HEAD)
        one = slice(at * HEAD, (at + 1) * HEAD)
        out[:ROWS, :] = keep[:ROWS, cols]
        out[ROWS:PAIR, :] = got[:ROWS, cols]
        out[PAIR:, :HEAD] = keep[ROWS:, one]
        out[PAIR:, HEAD:] = got[ROWS:, one]


def halves_kernel(where_ref, *refs):
    ins, (mine, theirs, sems) = refs[:3], refs[4:]
    copies = []
    for i, ref in enumerate(ins):
        cols = slice(i * HALF, (i + 1) * HALF)
        for side, out in ((where_ref[0], mine), (1 - where_ref[0], theirs)):
            start = pl.multiple_of(side * HALF, HALF)
            copies.append((ref.at[:, pl.ds(start, HALF)], out.at[:, cols]))
    fetched(copies, sems)


def total_kernel(where_ref, *refs):
    del where_ref
    refs[-1][...] = sum(r[...].astype(F32) for r in refs[:SLOTS]).astype(BF16)


def output_kernel(where_ref, own, cross, o, token, sems):
    side = where_ref[0]
    token[...] = jnp.zeros_like(token)
    fetched(
        [
            (part, o.at[:, pl.ds(pl.multiple_of(at * HALF, HALF), HALF)])
            for part, at in ((own, side), (cross, 1 - side))
        ],
        sems,
    )


def final_kernel(where_ref, *refs):
    side = where_ref[0]
    ins, (dq, dk, dv), sems = refs[:4], refs[5:8], refs[8]
    copies = []
    for i, at in enumerate((side, 1 - side)):
        wide = pl.ds(pl.multiple_of(at * HALF, HALF), HALF)
        head = pl.ds(pl.multiple_of(at * HEAD, HEAD), HEAD)
        copies.append((ins[i], dq.at[:, wide]))
        copies.append((ins[2 + i].at[:ROWS, :HEAD], dk.at[:, head]))
        copies.append((ins[2 + i].at[:ROWS, HEAD:], dv.at[:, head]))
    fetched(copies, sems)


def fill_cap(where_ref, blocks, cap):
    side, depth = where_ref[0], where_ref[1]
    segs = [b[PAIR : PAIR + 1, :].astype(F32) for b in blocks]
    start = jnp.zeros((1, PAIR), F32)
    for d in range(DOCS):
        first = jnp.sum((segs[0] < d).astype(F32), axis=1, keepdims=True)
        for k in range(1, SLOTS):
            same = jnp.sum((segs[k] == d).astype(F32), axis=1, keepdims=True)
            first = first - jnp.where(depth >= k, same, 0.0)
        start = jnp.where(segs[0] == d, first, start)
    start = start.astype(jnp.int32)
    lane = lax.broadcasted_iota(jnp.int32, (ROWS, PAIR), 1)
    row = jnp.where(lane < ROWS, lane + side * ROWS, lane - side * ROWS)
    for k in range(SLOTS):
        for part in range(2):
            block = side if part == 0 else 1 - side
            key = lax.broadcasted_iota(jnp.int32, (ROWS, PAIR), 0) + (block * ROWS - k * PAIR)
            seen = (key >= start) & (key <= row)
            cap[pl.ds(k * PAIR + part * ROWS, ROWS), :] = jnp.where(seen, 3.0e38, -jnp.inf)


def slot(k):
    return slice(k * PAIR, (k + 1) * PAIR)


def folded(x, reduce):
    return reduce(x.reshape(PAIR // 8, 8, PAIR), axis=0)


def joined(running, new, op):
    return new if running is None else op(running, new)


def bounded(k, s_ref, cap):
    return jnp.minimum(s_ref[slot(k), :], cap[slot(k), :])


def row_peak(s_ref, cap):
    peak = None
    for k in range(SLOTS):
        peak = joined(peak, folded(bounded(k, s_ref, cap), jnp.max), jnp.maximum)
    return jnp.max(peak, axis=0, keepdims=True)


def exponentials(k, s_ref, cap, peak):
    return jnp.exp2((bounded(k, s_ref, cap) - peak) * SCALE2)


def head_rows(own, crossed, g, offset=0):
    at = slice(offset + g * HEAD, offset + (g + 1) * HEAD)
    return jnp.concatenate([own[:, at], crossed[:, at]], axis=0)


def put_rows(g, columns, own, crossed):
    rows = columns.T.astype(BF16)
    at = slice(g * HEAD, (g + 1) * HEAD)
    own[:, at] = rows[:ROWS]
    crossed[:, at] = rows[ROWS:]


def fwd_kernel(where_ref, q_ref, qx_ref, *refs):
    blocks, refs = refs[:SLOTS], refs[SLOTS + 1 :]
    o_own, o_cross, cap, s_ref, e_ref, keys, vt_ref = refs
    fill_cap(where_ref, blocks, cap)
    for k, b in enumerate(blocks):
        keys[slot(k), :] = b[:PAIR, :HEAD]
        vt_ref[:, slot(k)] = b[:PAIR, HEAD:].T

    def score(g):
        s_ref[g % 2] = dot(keys[...], head_rows(q_ref, qx_ref, g, 2 * HALF).T)

    score(0)
    for g in range(GROUP):
        now = g % 2
        if g + 1 < GROUP:
            score(g + 1)
        top = row_peak(s_ref.at[now], cap)
        total = None
        for k in range(SLOTS):
            expo = exponentials(k, s_ref.at[now], cap, top)
            e_ref[now, slot(k), :] = expo.astype(BF16)
            total = joined(total, folded(expo, jnp.sum), jnp.add)
        inv = 1.0 / jnp.sum(total, axis=0, keepdims=True)
        put_rows(g, dot(vt_ref[...], e_ref[now]) * inv, o_own, o_cross)


def bwd_kernel(where_ref, qd_ref, qdx_ref, *refs):
    blocks, refs = refs[:SLOTS], refs[SLOTS:]
    dq_own, dq_cross = refs[:2]
    parts, refs = refs[2 : SLOTS + 2], refs[SLOTS + 2 :]
    cap, s_ref, dp_ref, e_ref, ds_ref, qs_ref, gs_ref, acc, keys, values, kt_ref, turned = refs
    fill_cap(where_ref, blocks, cap)
    for k, b in enumerate(blocks):
        keys[slot(k), :] = b[:PAIR, :HEAD]
        values[slot(k), :] = b[:PAIR, HEAD:]
        kt_ref[:, slot(k)] = b[:PAIR, :HEAD].T

    def rows_of(which, g):
        return head_rows(qd_ref, qdx_ref, g, which * HALF)

    def products(g):
        for i, (block, out) in enumerate(((keys, s_ref), (values, dp_ref))):
            turned[g % 2, i] = rows_of(i, g).T
            out[g % 2] = dot(block[...], turned[g % 2, i])

    def span_of(g, count=1):
        return slice(g * PAIR, (g + count) * PAIR)

    def key_terms(g):
        span = span_of(g, 2)
        both = dot_nt(qs_ref[:, span], ds_ref[:, span]), dot_nt(gs_ref[:, span], e_ref[:, span])
        for i, terms in enumerate(both):
            acc[i] = terms if g == 0 else acc[i] + terms

    products(0)
    for g in range(GROUP):
        now = g % 2
        cols = span_of(g)
        if g + 1 < GROUP:
            products(g + 1)
        if g > 1 and g % 2 == 0:
            key_terms(g - 2)
        top = row_peak(s_ref.at[now], cap)
        total = inner = None
        for k in range(SLOTS):
            expo = exponentials(k, s_ref.at[now], cap, top)
            e_ref[slot(k), cols] = expo.astype(BF16)
            total = joined(total, folded(expo, jnp.sum), jnp.add)
            inner = joined(inner, folded(expo * dp_ref[now, slot(k), :], jnp.sum), jnp.add)
        inv = 1.0 / jnp.sum(total, axis=0, keepdims=True)
        delta = jnp.sum(inner, axis=0, keepdims=True) * inv
        qs_ref[:, cols] = (turned[now, 0].astype(F32) * inv).astype(BF16)
        gs_ref[:, cols] = (turned[now, 1].astype(F32) * inv).astype(BF16)
        for k in range(SLOTS):
            ds = (dp_ref[now, slot(k), :] - delta).astype(BF16)
            ds_ref[slot(k), cols] = e_ref[slot(k), cols] * ds
        put_rows(g, dot(kt_ref[...], ds_ref[:, cols]) * (inv * SCALE), dq_own, dq_cross)
    key_terms(GROUP - 2)
    for k in range(SLOTS):
        parts[k][:, :HEAD] = (acc[0, :, slot(k)] * SCALE).T.astype(BF16)
        parts[k][:, HEAD:] = acc[1, :, slot(k)].T.astype(BF16)


MATMUL = 2 * GROUP * PAIR * KEYS * HEAD
FINAL_FLOPS = 2 * MATMUL


def run_fwd(where, own, crossed, blocks, after):
    scratch = [
        pltpu.VMEM((KEYS, PAIR), F32),
        pltpu.VMEM((2, KEYS, PAIR), F32),
        pltpu.VMEM((2, KEYS, PAIR), BF16),
        pltpu.VMEM((KEYS, HEAD), BF16),
        pltpu.VMEM((HEAD, KEYS), BF16),
    ]
    return call(
        fwd_kernel,
        [shape(ROWS, HALF)] * 2,
        [VMEM] * (2 + SLOTS) + [ANY] * 1,
        scratch,
        2 * MATMUL,
        2**21,
        "fwd",
        limit=20,
    )(where, own, crossed, *blocks, *after)


def run_bwd(where, own, crossed, blocks):
    outs = [shape(ROWS, HALF)] * 2 + [shape(PAIR, 2 * HEAD)] * SLOTS
    scratch = [
        pltpu.VMEM((KEYS, PAIR), F32),
        pltpu.VMEM((2, KEYS, PAIR), F32),
        pltpu.VMEM((2, KEYS, PAIR), F32),
        pltpu.VMEM((KEYS, GROUP * PAIR), BF16),
        pltpu.VMEM((KEYS, GROUP * PAIR), BF16),
        pltpu.VMEM((HEAD, GROUP * PAIR), BF16),
        pltpu.VMEM((HEAD, GROUP * PAIR), BF16),
        pltpu.VMEM((2, HEAD, KEYS), F32),
        pltpu.VMEM((KEYS, HEAD), BF16),
        pltpu.VMEM((KEYS, HEAD), BF16),
        pltpu.VMEM((HEAD, KEYS), BF16),
        pltpu.VMEM((2, 2, HEAD, PAIR), BF16),
    ]
    out = call(
        bwd_kernel,
        outs,
        2 + SLOTS,
        scratch,
        5 * MATMUL,
        2**22,
        "bwd",
        limit=32,
    )(where, own, crossed, *blocks)
    return out[0], out[1], out[2:]


def along_z(block, distance):
    n = lax.axis_size("cp")
    return lax.ppermute(block, "cp", [(i, (i + 2 * distance) % n) for i in range(n)])


def swapped(block):
    return lax.ppermute(block, "cp", [(i, i ^ 1) for i in range(lax.axis_size("cp"))])


def handed(block, distance):
    n = lax.axis_size("section")
    return lax.ppermute(block, "section", [(i, (i + distance) % n) for i in range(n)])


def handed_across(block, distance):
    n, m = lax.axis_size("section"), lax.axis_size("cp")
    route = [
        (s * m + c, (s + distance) % n * m + (c ^ 1)) for s in range(n) for c in range(m)
    ]
    return lax.ppermute(block, ("section", "cp"), route)


def split(where, *arrays):
    scratch = [
        pltpu.VMEM((4, ROWS, 2 * HEAD), BF16),
        pltpu.VMEM((2, 1, ROWS), jnp.int32),
        pltpu.SemaphoreType.DMA((6,)),
    ]
    outs = [shape(ROWS + TAIL, 4 * HEAD)] * 2
    return call(split_kernel, outs, [HBM] * 6, scratch, name="split")(where, *arrays)


def join(where, keep, got, through):
    return pl.pallas_call(
        join_kernel,
        out_shape=[shape(PAIR + TAIL, 2 * HEAD)] * 2 + [shape(*through.shape)],
        in_specs=[SMEM] + [VMEM] * 2 + [ANY],
        out_specs=[VMEM] * 2 + [ANY],
        input_output_aliases={3: 2},
        compiler_params=pltpu.CompilerParams(vmem_limit_bytes=4 * 2**20),
        name="join",
    )(where, keep, got, through)


def tied_kernel(where_ref, held, after, out):
    del where_ref, held, after, out


def tied(where, held, after):
    return pl.pallas_call(
        tied_kernel,
        out_shape=shape(*held.shape),
        in_specs=[SMEM, ANY, ANY],
        out_specs=ANY,
        input_output_aliases={1: 0},
        compiler_params=pltpu.CompilerParams(vmem_limit_bytes=2**20),
        name="tied",
    )(where, held, after)


def per_device(qf, kf, vf, sf, qb, kb, vb, sb, grad):
    index = lax.axis_index("cp")
    side = index % 2
    where = jnp.stack([side, index // 2]).astype(jnp.int32)
    qf, kf, vf, qb, kb, vb, grad = (a[0] for a in (qf, kf, vf, qb, kb, vb, grad))
    qf, kf, vf, sf, qb, kb, vb, sb, grad = (
        pltpu.with_memory_space_constraint(a, pltpu.HBM)
        for a in (qf, kf, vf, sf, qb, kb, vb, sb, grad)
    )

    keep, send = split(where, kb, vb, sb, kf, vf, sf)
    own, halves = call(
        halves_kernel,
        [shape(ROWS, 3 * HALF)] * 2,
        [HBM] * 3 + [ANY],
        [pltpu.SemaphoreType.DMA((6,))],
        name="halves",
    )(where, qb, grad, qf, send)
    b0, f0, halves = join(where, keep, swapped(send), halves)
    b4 = along_z(b0, -2)
    b2 = along_z(b0, 2)
    b1 = along_z(b0, 1)
    crossed = swapped(halves)
    b4 = along_z(b4, -2)
    b3 = along_z(b2, 1)
    f0 = tied(where, f0, b2)
    blocks_f = [f0] + [along_z(f0, k) for k in (1, 2, 3, 4)]

    dq_own, dq_cross, parts = run_bwd(where, own, crossed, (b0, b1, b2, b3, b4))
    four = along_z(parts[4], 2)
    terms = [parts[0]] + [along_z(parts[k], -k) for k in (1, 2, 3)] + [along_z(four, 2)]
    dq = handed(dq_own, -1), handed_across(dq_cross, -1)
    o_own, o_cross = run_fwd(where, own, crossed, blocks_f, (terms[1],))
    dq = handed(dq_own, -1), handed_across(dq_cross, -1)
    (summed,) = call(
        total_kernel, [shape(PAIR, 2 * HEAD)], [VMEM] * SLOTS + [ANY] * 2, name="total"
    )(where, *terms, *dq)
    received = handed(summed, -1)
    attn_out, token = call(
        output_kernel,
        [shape(ROWS, 2 * HALF), shape(TAIL, HEAD)],
        2,
        [pltpu.SemaphoreType.DMA((2,))],
        FINAL_FLOPS,
        name="output",
        place=[HBM, VMEM],
    )(where, handed(o_own, 1), handed_across(o_cross, 1))
    grads = call(
        final_kernel,
        [shape(ROWS, 2 * HALF)] + [shape(ROWS, 2 * HEAD)] * 2,
        [VMEM] * 4 + [ANY],
        [pltpu.SemaphoreType.DMA((6,))],
        name="final",
        place=HBM,
    )(where, *dq, received, swapped(received[ROWS:]), token)
    return tuple(out[None] for out in (attn_out, *grads))


def solution(mesh):
    wide = P("section", "cp", "tp")
    flat = P("section", "cp")
    return jax.shard_map(
        per_device,
        mesh=mesh,
        in_specs=(wide, wide, wide, flat, wide, wide, wide, flat, wide),
        out_specs=(wide, wide, wide, wide),
        check_vma=False,
    )
```

```python
import functools
import math

import jax
import jax.numpy as jnp
from jax import lax
from jax.experimental import pallas as pl
from jax.experimental.pallas import tpu as pltpu
from jax.sharding import PartitionSpec as P

HEAD = 128
ROWS = 128
GROUP = 8
PAIR = 2 * ROWS
SLOTS = 5
KEYS = SLOTS * PAIR
DOCS = 4
TAIL = 16
HALF = GROUP * HEAD
SCALE = HEAD ** (-0.5)
SCALE2 = SCALE * math.log2(math.e)
F32 = jnp.float32
BF16 = jnp.bfloat16
NT = (((1,), (1,)), ((), ()))
VMEM = pl.BlockSpec(memory_space=pltpu.VMEM)
SMEM = pl.BlockSpec(memory_space=pltpu.SMEM)
ANY = pl.BlockSpec(memory_space=pl.ANY)
HBM = pl.BlockSpec(memory_space=pltpu.HBM)


def dot(a, b):
    return jnp.dot(a, b, preferred_element_type=F32)


def dot_nt(a, b):
    return lax.dot_general(a, b, NT, preferred_element_type=F32)


def call(kernel, outs, ins, scratch=(), flops=0, moved_bytes=2**19, name=None, place=VMEM, limit=4):
    return pl.pallas_call(
        kernel,
        out_shape=outs,
        in_specs=[SMEM] + ([VMEM] * ins if isinstance(ins, int) else ins),
        out_specs=place if isinstance(place, list) else [place] * len(outs),
        scratch_shapes=scratch,
        compiler_params=pltpu.CompilerParams(vmem_limit_bytes=limit * 2**20),
        cost_estimate=pl.CostEstimate(flops=flops, bytes_accessed=moved_bytes, transcendentals=0),
        name=name,
    )


def shape(*dims):
    return jax.ShapeDtypeStruct(dims, BF16)


def fetched(copies, sems):
    started = [pltpu.make_async_copy(a, b, sems.at[i]) for i, (a, b) in enumerate(copies)]
    for c in started:
        c.start()
    for c in started:
        c.wait()


def split_kernel(where_ref, *refs):
    side = where_ref[0]
    ins, (keep, send, keys, segs, sems) = refs[:6], refs[6:]
    copies = []
    for i in range(2):
        copies += [(ins[3 * i], keys.at[2 * i]), (ins[3 * i + 1], keys.at[2 * i + 1])]
        copies.append((ins[3 * i + 2], segs.at[i]))
    fetched(copies, sems)
    for at in range(4):
        cols = slice(at * HEAD, (at + 1) * HEAD)
        low, high = keys[at, :, :HEAD], keys[at, :, HEAD:]
        keep[:ROWS, cols] = jnp.where(side == 0, low, high)
        send[:ROWS, cols] = jnp.where(side == 0, high, low)
        row = jnp.broadcast_to(segs[at // 2].astype(F32).astype(BF16), (TAIL, ROWS))
        for out in (keep, send):
            out[ROWS:, cols] = row


def join_kernel(where_ref, keep, got, half_in, eb, ef, half_out):
    del where_ref, half_in, half_out
    for at, out in ((0, eb), (2, ef)):
        cols = slice(at * HEAD, (at + 2) * HEAD)
        one = slice(at * HEAD, (at + 1) * HEAD)
        out[:ROWS, :] = keep[:ROWS, cols]
        out[ROWS:PAIR, :] = got[:ROWS, cols]
        out[PAIR:, :HEAD] = keep[ROWS:, one]
        out[PAIR:, HEAD:] = got[ROWS:, one]


def halves_kernel(where_ref, *refs):
    ins, (mine, theirs, sems) = refs[:3], refs[4:]
    copies = []
    for i, ref in enumerate(ins):
        cols = slice(i * HALF, (i + 1) * HALF)
        for side, out in ((where_ref[0], mine), (1 - where_ref[0], theirs)):
            start = pl.multiple_of(side * HALF, HALF)
            copies.append((ref.at[:, pl.ds(start, HALF)], out.at[:, cols]))
    fetched(copies, sems)


def total_kernel(where_ref, *refs):
    del where_ref
    refs[-1][...] = sum(r[...].astype(F32) for r in refs[:4]).astype(BF16)


def output_kernel(where_ref, own, cross, o, token, sems):
    side = where_ref[0]
    token[...] = jnp.zeros_like(token)
    fetched(
        [
            (part, o.at[:, pl.ds(pl.multiple_of(at * HALF, HALF), HALF)])
            for part, at in ((own, side), (cross, 1 - side))
        ],
        sems,
    )


def final_kernel(where_ref, *refs):
    side = where_ref[0]
    ins, (dq, dk, dv), sems = refs[:4], refs[5:8], refs[8]
    copies = []
    for i, at in enumerate((side, 1 - side)):
        wide = pl.ds(pl.multiple_of(at * HALF, HALF), HALF)
        head = pl.ds(pl.multiple_of(at * HEAD, HEAD), HEAD)
        copies.append((ins[i], dq.at[:, wide]))
        copies.append((ins[2 + i].at[:ROWS, :HEAD], dk.at[:, head]))
        copies.append((ins[2 + i].at[:ROWS, HEAD:], dv.at[:, head]))
    fetched(copies, sems)


def fill_cap(where_ref, blocks, cap):
    side, depth = where_ref[0], where_ref[1]
    segs = [b[PAIR : PAIR + 1, :].astype(F32) for b in blocks]
    start = jnp.zeros((1, PAIR), F32)
    for d in range(DOCS):
        first = jnp.sum((segs[0] < d).astype(F32), axis=1, keepdims=True)
        for k in range(1, SLOTS):
            same = jnp.sum((segs[k] == d).astype(F32), axis=1, keepdims=True)
            first = first - jnp.where(depth >= k, same, 0.0)
        start = jnp.where(segs[0] == d, first, start)
    start = start.astype(jnp.int32)
    lane = lax.broadcasted_iota(jnp.int32, (ROWS, PAIR), 1)
    row = jnp.where(lane < ROWS, lane + side * ROWS, lane - side * ROWS)
    for k in range(SLOTS):
        for part in range(2):
            block = side if part == 0 else 1 - side
            key = lax.broadcasted_iota(jnp.int32, (ROWS, PAIR), 0) + (block * ROWS - k * PAIR)
            seen = (key >= start) & (key <= row)
            cap[pl.ds(k * PAIR + part * ROWS, ROWS), :] = jnp.where(seen, 3.0e38, -jnp.inf)


def slot(k):
    return slice(k * PAIR, (k + 1) * PAIR)


def folded(x, reduce):
    return reduce(x.reshape(PAIR // 8, 8, PAIR), axis=0)


def joined(running, new, op):
    return new if running is None else op(running, new)


def bounded(k, s_ref, cap):
    return jnp.minimum(s_ref[slot(k), :], cap[slot(k), :])


def row_peak(s_ref, cap):
    peak = None
    for k in range(SLOTS):
        peak = joined(peak, folded(bounded(k, s_ref, cap), jnp.max), jnp.maximum)
    return jnp.max(peak, axis=0, keepdims=True)


def exponentials(k, s_ref, cap, peak):
    return jnp.exp2((bounded(k, s_ref, cap) - peak) * SCALE2)


def head_rows(own, crossed, g, offset=0):
    at = slice(offset + g * HEAD, offset + (g + 1) * HEAD)
    return jnp.concatenate([own[:, at], crossed[:, at]], axis=0)


def put_rows(g, columns, own, crossed):
    rows = columns.T.astype(BF16)
    at = slice(g * HEAD, (g + 1) * HEAD)
    own[:, at] = rows[:ROWS]
    crossed[:, at] = rows[ROWS:]


def fwd_kernel(where_ref, q_ref, qx_ref, *refs):
    blocks, refs = refs[:SLOTS], refs[SLOTS + 1 :]
    blocks = blocks[:1] + blocks[4:] + blocks[1:4]
    o_own, o_cross, cap, s_ref, e_ref, keys, vt_ref = refs
    fill_cap(where_ref, blocks, cap)
    for k, b in enumerate(blocks):
        keys[slot(k), :] = b[:PAIR, :HEAD]
        vt_ref[:, slot(k)] = b[:PAIR, HEAD:].T

    def score(g):
        s_ref[g % 2] = dot(keys[...], head_rows(q_ref, qx_ref, g, 2 * HALF).T)

    score(0)
    for g in range(GROUP):
        now = g % 2
        if g + 1 < GROUP:
            score(g + 1)
        top = row_peak(s_ref.at[now], cap)
        total = None
        for k in range(SLOTS):
            expo = exponentials(k, s_ref.at[now], cap, top)
            e_ref[now, slot(k), :] = expo.astype(BF16)
            total = joined(total, folded(expo, jnp.sum), jnp.add)
        inv = 1.0 / jnp.sum(total, axis=0, keepdims=True)
        put_rows(g, dot(vt_ref[...], e_ref[now]) * inv, o_own, o_cross)


def bwd_kernel(where_ref, qd_ref, qdx_ref, *refs):
    blocks, refs = refs[:SLOTS], refs[SLOTS:]
    dq_own, dq_cross = refs[:2]
    parts, refs = refs[2 : SLOTS + 2], refs[SLOTS + 2 :]
    cap, s_ref, dp_ref, e_ref, ds_ref, qs_ref, gs_ref, acc, keys, values, kt_ref, turned = refs
    fill_cap(where_ref, blocks, cap)
    for k, b in enumerate(blocks):
        keys[slot(k), :] = b[:PAIR, :HEAD]
        values[slot(k), :] = b[:PAIR, HEAD:]
        kt_ref[:, slot(k)] = b[:PAIR, :HEAD].T

    def rows_of(which, g):
        return head_rows(qd_ref, qdx_ref, g, which * HALF)

    def products(g):
        for i, (block, out) in enumerate(((keys, s_ref), (values, dp_ref))):
            turned[g % 2, i] = rows_of(i, g).T
            out[g % 2] = dot(block[...], turned[g % 2, i])

    def span_of(g, count=1):
        return slice(g * PAIR, (g + count) * PAIR)

    def key_terms(g):
        span = span_of(g, 2)
        both = dot_nt(qs_ref[:, span], ds_ref[:, span]), dot_nt(gs_ref[:, span], e_ref[:, span])
        for i, terms in enumerate(both):
            acc[i] = terms if g == 0 else acc[i] + terms

    products(0)
    for g in range(GROUP):
        now = g % 2
        cols = span_of(g)
        if g + 1 < GROUP:
            products(g + 1)
        if g > 1 and g % 2 == 0:
            key_terms(g - 2)
        top = row_peak(s_ref.at[now], cap)
        total = inner = None
        for k in range(SLOTS):
            expo = exponentials(k, s_ref.at[now], cap, top)
            e_ref[slot(k), cols] = expo.astype(BF16)
            total = joined(total, folded(expo, jnp.sum), jnp.add)
            inner = joined(inner, folded(expo * dp_ref[now, slot(k), :], jnp.sum), jnp.add)
        inv = 1.0 / jnp.sum(total, axis=0, keepdims=True)
        delta = jnp.sum(inner, axis=0, keepdims=True) * inv
        qs_ref[:, cols] = (turned[now, 0].astype(F32) * inv).astype(BF16)
        gs_ref[:, cols] = (turned[now, 1].astype(F32) * inv).astype(BF16)
        for k in range(SLOTS):
            ds = (dp_ref[now, slot(k), :] - delta).astype(BF16)
            ds_ref[slot(k), cols] = e_ref[slot(k), cols] * ds
        put_rows(g, dot(kt_ref[...], ds_ref[:, cols]) * (inv * SCALE), dq_own, dq_cross)
    key_terms(GROUP - 2)
    for k in range(SLOTS):
        parts[k][:, :HEAD] = (acc[0, :, slot(k)] * SCALE).T.astype(BF16)
        parts[k][:, HEAD:] = acc[1, :, slot(k)].T.astype(BF16)


MATMUL = 2 * GROUP * PAIR * KEYS * HEAD
FINAL_FLOPS = 2 * MATMUL


def run_fwd(where, own, crossed, blocks, after):
    scratch = [
        pltpu.VMEM((KEYS, PAIR), F32),
        pltpu.VMEM((2, KEYS, PAIR), F32),
        pltpu.VMEM((2, KEYS, PAIR), BF16),
        pltpu.VMEM((KEYS, HEAD), BF16),
        pltpu.VMEM((HEAD, KEYS), BF16),
    ]
    return call(
        fwd_kernel,
        [shape(ROWS, HALF)] * 2,
        [VMEM] * (2 + SLOTS) + [ANY] * 1,
        scratch,
        2 * MATMUL,
        2**21,
        "fwd",
        limit=20,
    )(where, own, crossed, *blocks, *after)


def run_bwd(where, own, crossed, blocks):
    outs = [shape(ROWS, HALF)] * 2 + [shape(PAIR, 2 * HEAD)] * SLOTS
    scratch = [
        pltpu.VMEM((KEYS, PAIR), F32),
        pltpu.VMEM((2, KEYS, PAIR), F32),
        pltpu.VMEM((2, KEYS, PAIR), F32),
        pltpu.VMEM((KEYS, GROUP * PAIR), BF16),
        pltpu.VMEM((KEYS, GROUP * PAIR), BF16),
        pltpu.VMEM((HEAD, GROUP * PAIR), BF16),
        pltpu.VMEM((HEAD, GROUP * PAIR), BF16),
        pltpu.VMEM((2, HEAD, KEYS), F32),
        pltpu.VMEM((KEYS, HEAD), BF16),
        pltpu.VMEM((KEYS, HEAD), BF16),
        pltpu.VMEM((HEAD, KEYS), BF16),
        pltpu.VMEM((2, 2, HEAD, PAIR), BF16),
    ]
    out = call(
        bwd_kernel,
        outs,
        2 + SLOTS,
        scratch,
        5 * MATMUL,
        2**22,
        "bwd",
        limit=32,
    )(where, own, crossed, *blocks)
    return out[0], out[1], out[2:]


def along_z(block, distance):
    n = lax.axis_size("cp")
    return lax.ppermute(block, "cp", [(i, (i + 2 * distance) % n) for i in range(n)])


def swapped(block):
    return lax.ppermute(block, "cp", [(i, i ^ 1) for i in range(lax.axis_size("cp"))])


def handed(block, distance):
    n = lax.axis_size("section")
    return lax.ppermute(block, "section", [(i, (i + distance) % n) for i in range(n)])


def handed_across(block, distance):
    n, m = lax.axis_size("section"), lax.axis_size("cp")
    route = [
        (s * m + c, (s + distance) % n * m + (c ^ 1)) for s in range(n) for c in range(m)
    ]
    return lax.ppermute(block, ("section", "cp"), route)


def split(where, *arrays):
    scratch = [
        pltpu.VMEM((4, ROWS, 2 * HEAD), BF16),
        pltpu.VMEM((2, 1, ROWS), jnp.int32),
        pltpu.SemaphoreType.DMA((6,)),
    ]
    outs = [shape(ROWS + TAIL, 4 * HEAD)] * 2
    return call(split_kernel, outs, [HBM] * 6, scratch, name="split")(where, *arrays)


def join(where, keep, got, through):
    return pl.pallas_call(
        join_kernel,
        out_shape=[shape(PAIR + TAIL, 2 * HEAD)] * 2 + [shape(*through.shape)],
        in_specs=[SMEM] + [VMEM] * 2 + [ANY],
        out_specs=[VMEM] * 2 + [ANY],
        input_output_aliases={3: 2},
        compiler_params=pltpu.CompilerParams(vmem_limit_bytes=4 * 2**20),
        name="join",
    )(where, keep, got, through)


def tied_kernel(where_ref, held, after, out):
    del where_ref, held, after, out


def tied(where, held, after):
    return pl.pallas_call(
        tied_kernel,
        out_shape=shape(*held.shape),
        in_specs=[SMEM, ANY, ANY],
        out_specs=ANY,
        input_output_aliases={1: 0},
        compiler_params=pltpu.CompilerParams(vmem_limit_bytes=2**20),
        name="tied",
    )(where, held, after)


def per_device(qf, kf, vf, sf, qb, kb, vb, sb, grad):
    index = lax.axis_index("cp")
    side = index % 2
    where = jnp.stack([side, index // 2]).astype(jnp.int32)
    qf, kf, vf, qb, kb, vb, grad = (a[0] for a in (qf, kf, vf, qb, kb, vb, grad))
    qf, kf, vf, sf, qb, kb, vb, sb, grad = (
        pltpu.with_memory_space_constraint(a, pltpu.HBM)
        for a in (qf, kf, vf, sf, qb, kb, vb, sb, grad)
    )

    keep, send = split(where, kb, vb, sb, kf, vf, sf)
    own, halves = call(
        halves_kernel,
        [shape(ROWS, 3 * HALF)] * 2,
        [HBM] * 3 + [ANY],
        [pltpu.SemaphoreType.DMA((6,))],
        name="halves",
    )(where, qb, grad, qf, send)
    b0, f0, halves = join(where, keep, swapped(send), halves)
    b4 = along_z(b0, -2)
    b2 = along_z(b0, 2)
    b1 = along_z(b0, 1)
    crossed = swapped(halves)
    b4 = along_z(b4, -2)
    b3 = along_z(b2, 1)
    f0 = tied(where, f0, b2)
    f4, f3, f2, f1 = (along_z(f0, k) for k in (4, 3, 2, 1))
    blocks_f = (f0, f2, f3, f4, f1)

    dq_own, dq_cross, parts = run_bwd(where, own, crossed, (b0, b1, b2, b3, b4))
    far = along_z(parts[4], -1)
    three = (parts[3].astype(F32) + far.astype(F32)).astype(BF16)
    terms = [parts[0]] + [along_z(parts[k], -k) for k in (1, 2)] + [along_z(three, -3)]
    dq = handed(dq_own, -1), handed_across(dq_cross, -1)
    o_own, o_cross = run_fwd(where, own, crossed, blocks_f, (terms[1],))
    dq = handed(dq_own, -1), handed_across(dq_cross, -1)
    (summed,) = call(
        total_kernel, [shape(PAIR, 2 * HEAD)], [VMEM] * 4 + [ANY] * 2, name="total"
    )(where, *terms, *dq)
    received = handed(summed, -1)
    attn_out, token = call(
        output_kernel,
        [shape(ROWS, 2 * HALF), shape(TAIL, HEAD)],
        2,
        [pltpu.SemaphoreType.DMA((2,))],
        FINAL_FLOPS,
        name="output",
        place=[HBM, VMEM],
    )(where, handed(o_own, 1), handed_across(o_cross, 1))
    grads = call(
        final_kernel,
        [shape(ROWS, 2 * HALF)] + [shape(ROWS, 2 * HEAD)] * 2,
        [VMEM] * 4 + [ANY],
        [pltpu.SemaphoreType.DMA((6,))],
        name="final",
        place=HBM,
    )(where, *dq, received, swapped(received[ROWS:]), token)
    return tuple(out[None] for out in (attn_out, *grads))


def solution(mesh):
    wide = P("section", "cp", "tp")
    flat = P("section", "cp")
    return jax.shard_map(
        per_device,
        mesh=mesh,
        in_specs=(wide, wide, wide, flat, wide, wide, wide, flat, wide),
        out_specs=(wide, wide, wide, wide),
        check_vma=False,
    )
```

```python
import functools
import math

import jax
import jax.numpy as jnp
from jax import lax
from jax.experimental import pallas as pl
from jax.experimental.pallas import tpu as pltpu
from jax.sharding import PartitionSpec as P

HEAD = 128
ROWS = 128
GROUP = 8
PAIR = 2 * ROWS
SLOTS = 5
KEYS = SLOTS * PAIR
DOCS = 4
TAIL = 16
HALF = GROUP * HEAD
SCALE = HEAD ** (-0.5)
SCALE2 = SCALE * math.log2(math.e)
F32 = jnp.float32
BF16 = jnp.bfloat16
NT = (((1,), (1,)), ((), ()))
VMEM = pl.BlockSpec(memory_space=pltpu.VMEM)
SMEM = pl.BlockSpec(memory_space=pltpu.SMEM)
ANY = pl.BlockSpec(memory_space=pl.ANY)
HBM = pl.BlockSpec(memory_space=pltpu.HBM)


def dot(a, b):
    return jnp.dot(a, b, preferred_element_type=F32)


def dot_nt(a, b):
    return lax.dot_general(a, b, NT, preferred_element_type=F32)


def call(kernel, outs, ins, scratch=(), flops=0, moved_bytes=2**19, name=None, place=VMEM, limit=4):
    return pl.pallas_call(
        kernel,
        out_shape=outs,
        in_specs=[SMEM] + ([VMEM] * ins if isinstance(ins, int) else ins),
        out_specs=place if isinstance(place, list) else [place] * len(outs),
        scratch_shapes=scratch,
        compiler_params=pltpu.CompilerParams(vmem_limit_bytes=limit * 2**20),
        cost_estimate=pl.CostEstimate(flops=flops, bytes_accessed=moved_bytes, transcendentals=0),
        name=name,
    )


def shape(*dims):
    return jax.ShapeDtypeStruct(dims, BF16)


def fetched(copies, sems):
    started = [pltpu.make_async_copy(a, b, sems.at[i]) for i, (a, b) in enumerate(copies)]
    for c in started:
        c.start()
    for c in started:
        c.wait()


def split_kernel(where_ref, *refs):
    side = where_ref[0]
    ins, (keep, send, keys, segs, sems) = refs[:6], refs[6:]
    copies = []
    for i in range(2):
        copies += [(ins[3 * i], keys.at[2 * i]), (ins[3 * i + 1], keys.at[2 * i + 1])]
        copies.append((ins[3 * i + 2], segs.at[i]))
    fetched(copies, sems)
    for at in range(4):
        cols = slice(at * HEAD, (at + 1) * HEAD)
        low, high = keys[at, :, :HEAD], keys[at, :, HEAD:]
        keep[:ROWS, cols] = jnp.where(side == 0, low, high)
        send[:ROWS, cols] = jnp.where(side == 0, high, low)
        row = jnp.broadcast_to(segs[at // 2].astype(F32).astype(BF16), (TAIL, ROWS))
        for out in (keep, send):
            out[ROWS:, cols] = row


def join_kernel(where_ref, keep, got, half_in, eb, ef, half_out):
    del where_ref, half_in, half_out
    for at, out in ((0, eb), (2, ef)):
        cols = slice(at * HEAD, (at + 2) * HEAD)
        one = slice(at * HEAD, (at + 1) * HEAD)
        out[:ROWS, :] = keep[:ROWS, cols]
        out[ROWS:PAIR, :] = got[:ROWS, cols]
        out[PAIR:, :HEAD] = keep[ROWS:, one]
        out[PAIR:, HEAD:] = got[ROWS:, one]


def halves_kernel(where_ref, *refs):
    ins, (mine, theirs, sems) = refs[:3], refs[4:]
    copies = []
    for i, ref in enumerate(ins):
        cols = slice(i * HALF, (i + 1) * HALF)
        for side, out in ((where_ref[0], mine), (1 - where_ref[0], theirs)):
            start = pl.multiple_of(side * HALF, HALF)
            copies.append((ref.at[:, pl.ds(start, HALF)], out.at[:, cols]))
    fetched(copies, sems)


def total_kernel(where_ref, *refs):
    del where_ref
    refs[-1][...] = sum(r[...].astype(F32) for r in refs[:4]).astype(BF16)


def output_kernel(where_ref, own, cross, o, token, sems):
    side = where_ref[0]
    token[...] = jnp.zeros_like(token)
    fetched(
        [
            (part, o.at[:, pl.ds(pl.multiple_of(at * HALF, HALF), HALF)])
            for part, at in ((own, side), (cross, 1 - side))
        ],
        sems,
    )


def final_kernel(where_ref, *refs):
    side = where_ref[0]
    ins, (dq, dk, dv), sems = refs[:4], refs[5:8], refs[8]
    copies = []
    for i, at in enumerate((side, 1 - side)):
        wide = pl.ds(pl.multiple_of(at * HALF, HALF), HALF)
        head = pl.ds(pl.multiple_of(at * HEAD, HEAD), HEAD)
        copies.append((ins[i], dq.at[:, wide]))
        copies.append((ins[2 + i].at[:ROWS, :HEAD], dk.at[:, head]))
        copies.append((ins[2 + i].at[:ROWS, HEAD:], dv.at[:, head]))
    fetched(copies, sems)


def fill_cap(where_ref, blocks, cap):
    side, depth = where_ref[0], where_ref[1]
    segs = [b[PAIR : PAIR + 1, :].astype(F32) for b in blocks]
    start = jnp.zeros((1, PAIR), F32)
    for d in range(DOCS):
        first = jnp.sum((segs[0] < d).astype(F32), axis=1, keepdims=True)
        for k in range(1, SLOTS):
            same = jnp.sum((segs[k] == d).astype(F32), axis=1, keepdims=True)
            first = first - jnp.where(depth >= k, same, 0.0)
        start = jnp.where(segs[0] == d, first, start)
    start = start.astype(jnp.int32)
    lane = lax.broadcasted_iota(jnp.int32, (ROWS, PAIR), 1)
    row = jnp.where(lane < ROWS, lane + side * ROWS, lane - side * ROWS)
    for k in range(SLOTS):
        for part in range(2):
            block = side if part == 0 else 1 - side
            key = lax.broadcasted_iota(jnp.int32, (ROWS, PAIR), 0) + (block * ROWS - k * PAIR)
            seen = (key >= start) & (key <= row)
            cap[pl.ds(k * PAIR + part * ROWS, ROWS), :] = jnp.where(seen, 3.0e38, -jnp.inf)


def slot(k):
    return slice(k * PAIR, (k + 1) * PAIR)


def folded(x, reduce):
    return reduce(x.reshape(PAIR // 8, 8, PAIR), axis=0)


def joined(running, new, op):
    return new if running is None else op(running, new)


def bounded(k, s_ref, cap):
    return jnp.minimum(s_ref[slot(k), :], cap[slot(k), :])


def row_peak(s_ref, cap):
    peak = None
    for k in range(SLOTS):
        peak = joined(peak, folded(bounded(k, s_ref, cap), jnp.max), jnp.maximum)
    return jnp.max(peak, axis=0, keepdims=True)


def exponentials(k, s_ref, cap, peak):
    return jnp.exp2((bounded(k, s_ref, cap) - peak) * SCALE2)


def head_rows(own, crossed, g, offset=0):
    at = slice(offset + g * HEAD, offset + (g + 1) * HEAD)
    return jnp.concatenate([own[:, at], crossed[:, at]], axis=0)


def put_rows(g, columns, own, crossed):
    rows = columns.T.astype(BF16)
    at = slice(g * HEAD, (g + 1) * HEAD)
    own[:, at] = rows[:ROWS]
    crossed[:, at] = rows[ROWS:]


def fwd_kernel(where_ref, q_ref, qx_ref, *refs):
    blocks, refs = refs[:SLOTS], refs[SLOTS + 1 :]
    blocks = blocks[:1] + blocks[4:] + blocks[1:4]
    o_own, o_cross, cap, s_ref, e_ref, keys, vt_ref = refs
    fill_cap(where_ref, blocks, cap)
    for k, b in enumerate(blocks):
        keys[slot(k), :] = b[:PAIR, :HEAD]
        vt_ref[:, slot(k)] = b[:PAIR, HEAD:].T

    def score(g):
        s_ref[g % 2] = dot(keys[...], head_rows(q_ref, qx_ref, g, 2 * HALF).T)

    score(0)
    for g in range(GROUP):
        now = g % 2
        if g + 1 < GROUP:
            score(g + 1)
        top = row_peak(s_ref.at[now], cap)
        total = None
        for k in range(SLOTS):
            expo = exponentials(k, s_ref.at[now], cap, top)
            e_ref[now, slot(k), :] = expo.astype(BF16)
            total = joined(total, folded(expo, jnp.sum), jnp.add)
        inv = 1.0 / jnp.sum(total, axis=0, keepdims=True)
        put_rows(g, dot(vt_ref[...], e_ref[now]) * inv, o_own, o_cross)


def bwd_kernel(where_ref, qd_ref, qdx_ref, *refs):
    blocks, refs = refs[:SLOTS], refs[SLOTS:]
    dq_own, dq_cross = refs[:2]
    parts, refs = refs[2 : SLOTS + 2], refs[SLOTS + 2 :]
    cap, s_ref, dp_ref, e_ref, ds_ref, qs_ref, gs_ref, acc, keys, values, kt_ref, turned = refs
    fill_cap(where_ref, blocks, cap)
    for k, b in enumerate(blocks):
        keys[slot(k), :] = b[:PAIR, :HEAD]
        values[slot(k), :] = b[:PAIR, HEAD:]
        kt_ref[:, slot(k)] = b[:PAIR, :HEAD].T

    def rows_of(which, g):
        return head_rows(qd_ref, qdx_ref, g, which * HALF)

    def products(g):
        for i, (block, out) in enumerate(((keys, s_ref), (values, dp_ref))):
            turned[g % 2, i] = rows_of(i, g).T
            out[g % 2] = dot(block[...], turned[g % 2, i])

    def span_of(g, count=1):
        return slice(g * PAIR, (g + count) * PAIR)

    def key_terms(g):
        span = span_of(g, 2)
        both = dot_nt(qs_ref[:, span], ds_ref[:, span]), dot_nt(gs_ref[:, span], e_ref[:, span])
        for i, terms in enumerate(both):
            acc[i] = terms if g == 0 else acc[i] + terms

    products(0)
    for g in range(GROUP):
        now = g % 2
        cols = span_of(g)
        if g + 1 < GROUP:
            products(g + 1)
        if g > 1 and g % 2 == 0:
            key_terms(g - 2)
        top = row_peak(s_ref.at[now], cap)
        total = inner = None
        for k in range(SLOTS):
            expo = exponentials(k, s_ref.at[now], cap, top)
            e_ref[slot(k), cols] = expo.astype(BF16)
            total = joined(total, folded(expo, jnp.sum), jnp.add)
            inner = joined(inner, folded(expo * dp_ref[now, slot(k), :], jnp.sum), jnp.add)
        inv = 1.0 / jnp.sum(total, axis=0, keepdims=True)
        delta = jnp.sum(inner, axis=0, keepdims=True) * inv
        qs_ref[:, cols] = (turned[now, 0].astype(F32) * inv).astype(BF16)
        gs_ref[:, cols] = (turned[now, 1].astype(F32) * inv).astype(BF16)
        for k in range(SLOTS):
            ds = (dp_ref[now, slot(k), :] - delta).astype(BF16)
            ds_ref[slot(k), cols] = e_ref[slot(k), cols] * ds
        put_rows(g, dot(kt_ref[...], ds_ref[:, cols]) * (inv * SCALE), dq_own, dq_cross)
    key_terms(GROUP - 2)
    for k in range(SLOTS):
        parts[k][:, :HEAD] = (acc[0, :, slot(k)] * SCALE).T.astype(BF16)
        parts[k][:, HEAD:] = acc[1, :, slot(k)].T.astype(BF16)


MATMUL = 2 * GROUP * PAIR * KEYS * HEAD
FINAL_FLOPS = 2 * MATMUL


def run_fwd(where, own, crossed, blocks, after):
    scratch = [
        pltpu.VMEM((KEYS, PAIR), F32),
        pltpu.VMEM((2, KEYS, PAIR), F32),
        pltpu.VMEM((2, KEYS, PAIR), BF16),
        pltpu.VMEM((KEYS, HEAD), BF16),
        pltpu.VMEM((HEAD, KEYS), BF16),
    ]
    return call(
        fwd_kernel,
        [shape(ROWS, HALF)] * 2,
        [VMEM] * (2 + SLOTS) + [ANY] * 1,
        scratch,
        2 * MATMUL,
        2**21,
        "fwd",
        limit=20,
    )(where, own, crossed, *blocks, *after)


def run_bwd(where, own, crossed, blocks):
    outs = [shape(ROWS, HALF)] * 2 + [shape(PAIR, 2 * HEAD)] * SLOTS
    scratch = [
        pltpu.VMEM((KEYS, PAIR), F32),
        pltpu.VMEM((2, KEYS, PAIR), F32),
        pltpu.VMEM((2, KEYS, PAIR), F32),
        pltpu.VMEM((KEYS, GROUP * PAIR), BF16),
        pltpu.VMEM((KEYS, GROUP * PAIR), BF16),
        pltpu.VMEM((HEAD, GROUP * PAIR), BF16),
        pltpu.VMEM((HEAD, GROUP * PAIR), BF16),
        pltpu.VMEM((2, HEAD, KEYS), F32),
        pltpu.VMEM((KEYS, HEAD), BF16),
        pltpu.VMEM((KEYS, HEAD), BF16),
        pltpu.VMEM((HEAD, KEYS), BF16),
        pltpu.VMEM((2, 2, HEAD, PAIR), BF16),
    ]
    out = call(
        bwd_kernel,
        outs,
        2 + SLOTS,
        scratch,
        5 * MATMUL,
        2**22,
        "bwd",
        limit=32,
    )(where, own, crossed, *blocks)
    return out[0], out[1], out[2:]


def along_z(block, distance):
    n = lax.axis_size("cp")
    return lax.ppermute(block, "cp", [(i, (i + 2 * distance) % n) for i in range(n)])


def swapped(block):
    return lax.ppermute(block, "cp", [(i, i ^ 1) for i in range(lax.axis_size("cp"))])


def handed(block, distance):
    n = lax.axis_size("section")
    return lax.ppermute(block, "section", [(i, (i + distance) % n) for i in range(n)])


def handed_across(block, distance):
    n, m = lax.axis_size("section"), lax.axis_size("cp")
    route = [
        (s * m + c, (s + distance) % n * m + (c ^ 1)) for s in range(n) for c in range(m)
    ]
    return lax.ppermute(block, ("section", "cp"), route)


def split(where, *arrays):
    scratch = [
        pltpu.VMEM((4, ROWS, 2 * HEAD), BF16),
        pltpu.VMEM((2, 1, ROWS), jnp.int32),
        pltpu.SemaphoreType.DMA((6,)),
    ]
    outs = [shape(ROWS + TAIL, 4 * HEAD)] * 2
    return call(split_kernel, outs, [HBM] * 6, scratch, name="split")(where, *arrays)


def join(where, keep, got, through):
    return pl.pallas_call(
        join_kernel,
        out_shape=[shape(PAIR + TAIL, 2 * HEAD)] * 2 + [shape(*through.shape)],
        in_specs=[SMEM] + [VMEM] * 2 + [ANY],
        out_specs=[VMEM] * 2 + [ANY],
        input_output_aliases={3: 2},
        compiler_params=pltpu.CompilerParams(vmem_limit_bytes=4 * 2**20),
        name="join",
    )(where, keep, got, through)


def tied_kernel(where_ref, held, after, out):
    del where_ref, held, after, out


def tied(where, held, after):
    return pl.pallas_call(
        tied_kernel,
        out_shape=shape(*held.shape),
        in_specs=[SMEM, ANY, ANY],
        out_specs=ANY,
        input_output_aliases={1: 0},
        compiler_params=pltpu.CompilerParams(vmem_limit_bytes=2**20),
        name="tied",
    )(where, held, after)


def per_device(qf, kf, vf, sf, qb, kb, vb, sb, grad):
    index = lax.axis_index("cp")
    side = index % 2
    where = jnp.stack([side, index // 2]).astype(jnp.int32)
    qf, kf, vf, qb, kb, vb, grad = (a[0] for a in (qf, kf, vf, qb, kb, vb, grad))
    qf, kf, vf, sf, qb, kb, vb, sb, grad = (
        pltpu.with_memory_space_constraint(a, pltpu.HBM)
        for a in (qf, kf, vf, sf, qb, kb, vb, sb, grad)
    )

    keep, send = split(where, kb, vb, sb, kf, vf, sf)
    own, halves = call(
        halves_kernel,
        [shape(ROWS, 3 * HALF)] * 2,
        [HBM] * 3 + [ANY],
        [pltpu.SemaphoreType.DMA((6,))],
        name="halves",
    )(where, qb, grad, qf, send)
    b0, f0, halves = join(where, keep, swapped(send), halves)
    b4 = along_z(b0, -2)
    b2 = along_z(b0, 2)
    b1 = along_z(b0, 1)
    crossed = swapped(halves)
    b4 = along_z(b4, -2)
    b3 = along_z(b2, 1)
    f0 = tied(where, f0, b2)
    f4, f3, f2, f1 = (along_z(f0, k) for k in (4, 3, 2, 1))
    blocks_f = (f0, f2, f3, f4, f1)

    dq_own, dq_cross, parts = run_bwd(where, own, crossed, (b0, b1, b2, b3, b4))
    far = along_z(parts[4], -1)
    three = (parts[3].astype(F32) + far.astype(F32)).astype(BF16)
    terms = [parts[0]] + [along_z(parts[k], -k) for k in (1, 2)] + [along_z(three, -3)]
    dq = handed(dq_own, -1), handed_across(dq_cross, -1)
    o_own, o_cross = run_fwd(where, own, crossed, blocks_f, (three,))
    dq = handed(dq_own, -1), handed_across(dq_cross, -1)
    (summed,) = call(
        total_kernel, [shape(PAIR, 2 * HEAD)], [VMEM] * 4 + [ANY] * 2, name="total"
    )(where, *terms, *dq)
    received = handed(summed, -1)
    attn_out, token = call(
        output_kernel,
        [shape(ROWS, 2 * HALF), shape(TAIL, HEAD)],
        2,
        [pltpu.SemaphoreType.DMA((2,))],
        FINAL_FLOPS,
        name="output",
        place=[HBM, VMEM],
    )(where, handed(o_own, 1), handed_across(o_cross, 1))
    grads = call(
        final_kernel,
        [shape(ROWS, 2 * HALF)] + [shape(ROWS, 2 * HEAD)] * 2,
        [VMEM] * 4 + [ANY],
        [pltpu.SemaphoreType.DMA((6,))],
        name="final",
        place=HBM,
    )(where, *dq, received, swapped(received[ROWS:]), token)
    return tuple(out[None] for out in (attn_out, *grads))


def solution(mesh):
    wide = P("section", "cp", "tp")
    flat = P("section", "cp")
    return jax.shard_map(
        per_device,
        mesh=mesh,
        in_specs=(wide, wide, wide, flat, wide, wide, wide, flat, wide),
        out_specs=(wide, wide, wide, wide),
        check_vma=False,
    )
```

```python
import functools
import math

import jax
import jax.numpy as jnp
from jax import lax
from jax.experimental import pallas as pl
from jax.experimental.pallas import tpu as pltpu
from jax.sharding import PartitionSpec as P

HEAD = 128
ROWS = 128
GROUP = 8
PAIR = 2 * ROWS
SLOTS = 5
KEYS = SLOTS * PAIR
DOCS = 4
TAIL = 16
HALF = GROUP * HEAD
SCALE = HEAD ** (-0.5)
SCALE2 = SCALE * math.log2(math.e)
F32 = jnp.float32
BF16 = jnp.bfloat16
NT = (((1,), (1,)), ((), ()))
VMEM = pl.BlockSpec(memory_space=pltpu.VMEM)
SMEM = pl.BlockSpec(memory_space=pltpu.SMEM)
ANY = pl.BlockSpec(memory_space=pl.ANY)
HBM = pl.BlockSpec(memory_space=pltpu.HBM)


def dot(a, b):
    return jnp.dot(a, b, preferred_element_type=F32)


def dot_nt(a, b):
    return lax.dot_general(a, b, NT, preferred_element_type=F32)


def call(kernel, outs, ins, scratch=(), flops=0, moved_bytes=2**19, name=None, place=VMEM, limit=4):
    return pl.pallas_call(
        kernel,
        out_shape=outs,
        in_specs=[SMEM] + ([VMEM] * ins if isinstance(ins, int) else ins),
        out_specs=place if isinstance(place, list) else [place] * len(outs),
        scratch_shapes=scratch,
        compiler_params=pltpu.CompilerParams(vmem_limit_bytes=limit * 2**20),
        cost_estimate=pl.CostEstimate(flops=flops, bytes_accessed=moved_bytes, transcendentals=0),
        name=name,
    )


def shape(*dims):
    return jax.ShapeDtypeStruct(dims, BF16)


def fetched(copies, sems):
    started = [pltpu.make_async_copy(a, b, sems.at[i]) for i, (a, b) in enumerate(copies)]
    for c in started:
        c.start()
    for c in started:
        c.wait()


def split_kernel(where_ref, *refs):
    side = where_ref[0]
    ins, (keep, send, keys, segs, sems) = refs[:6], refs[6:]
    copies = []
    for i in range(2):
        copies += [(ins[3 * i], keys.at[2 * i]), (ins[3 * i + 1], keys.at[2 * i + 1])]
        copies.append((ins[3 * i + 2], segs.at[i]))
    fetched(copies, sems)
    for at in range(4):
        cols = slice(at * HEAD, (at + 1) * HEAD)
        low, high = keys[at, :, :HEAD], keys[at, :, HEAD:]
        keep[:ROWS, cols] = jnp.where(side == 0, low, high)
        send[:ROWS, cols] = jnp.where(side == 0, high, low)
        row = jnp.broadcast_to(segs[at // 2].astype(F32).astype(BF16), (TAIL, ROWS))
        for out in (keep, send):
            out[ROWS:, cols] = row


def join_kernel(where_ref, keep, got, half_in, eb, ef, half_out):
    del where_ref, half_in, half_out
    for at, out in ((0, eb), (2, ef)):
        cols = slice(at * HEAD, (at + 2) * HEAD)
        one = slice(at * HEAD, (at + 1) * HEAD)
        out[:ROWS, :] = keep[:ROWS, cols]
        out[ROWS:PAIR, :] = got[:ROWS, cols]
        out[PAIR:, :HEAD] = keep[ROWS:, one]
        out[PAIR:, HEAD:] = got[ROWS:, one]


def halves_kernel(where_ref, *refs):
    ins, (mine, theirs, sems) = refs[:3], refs[4:]
    copies = []
    for i, ref in enumerate(ins):
        cols = slice(i * HALF, (i + 1) * HALF)
        for side, out in ((where_ref[0], mine), (1 - where_ref[0], theirs)):
            start = pl.multiple_of(side * HALF, HALF)
            copies.append((ref.at[:, pl.ds(start, HALF)], out.at[:, cols]))
    fetched(copies, sems)


def total_kernel(where_ref, *refs):
    del where_ref
    refs[-1][...] = sum(r[...].astype(F32) for r in refs[:4]).astype(BF16)


def output_kernel(where_ref, own, cross, o, token, sems):
    side = where_ref[0]
    token[...] = jnp.zeros_like(token)
    fetched(
        [
            (part, o.at[:, pl.ds(pl.multiple_of(at * HALF, HALF), HALF)])
            for part, at in ((own, side), (cross, 1 - side))
        ],
        sems,
    )


def final_kernel(where_ref, *refs):
    side = where_ref[0]
    ins, (dq, dk, dv), sems = refs[:4], refs[5:8], refs[8]
    copies = []
    for i, at in enumerate((side, 1 - side)):
        wide = pl.ds(pl.multiple_of(at * HALF, HALF), HALF)
        head = pl.ds(pl.multiple_of(at * HEAD, HEAD), HEAD)
        copies.append((ins[i], dq.at[:, wide]))
        copies.append((ins[2 + i].at[:ROWS, :HEAD], dk.at[:, head]))
        copies.append((ins[2 + i].at[:ROWS, HEAD:], dv.at[:, head]))
    fetched(copies, sems)


def fill_cap(where_ref, blocks, cap):
    side, depth = where_ref[0], where_ref[1]
    segs = [b[PAIR : PAIR + 1, :].astype(F32) for b in blocks]
    start = jnp.zeros((1, PAIR), F32)
    for d in range(DOCS):
        first = jnp.sum((segs[0] < d).astype(F32), axis=1, keepdims=True)
        for k in range(1, SLOTS):
            same = jnp.sum((segs[k] == d).astype(F32), axis=1, keepdims=True)
            first = first - jnp.where(depth >= k, same, 0.0)
        start = jnp.where(segs[0] == d, first, start)
    start = start.astype(jnp.int32)
    lane = lax.broadcasted_iota(jnp.int32, (ROWS, PAIR), 1)
    row = jnp.where(lane < ROWS, lane + side * ROWS, lane - side * ROWS)
    for k in range(SLOTS):
        for part in range(2):
            block = side if part == 0 else 1 - side
            key = lax.broadcasted_iota(jnp.int32, (ROWS, PAIR), 0) + (block * ROWS - k * PAIR)
            seen = (key >= start) & (key <= row)
            cap[pl.ds(k * PAIR + part * ROWS, ROWS), :] = jnp.where(seen, 3.0e38, -jnp.inf)


def slot(k):
    return slice(k * PAIR, (k + 1) * PAIR)


def folded(x, reduce):
    return reduce(x.reshape(PAIR // 8, 8, PAIR), axis=0)


def joined(running, new, op):
    return new if running is None else op(running, new)


def bounded(k, s_ref, cap):
    return jnp.minimum(s_ref[slot(k), :], cap[slot(k), :])


def row_peak(s_ref, cap):
    peak = None
    for k in range(SLOTS):
        peak = joined(peak, folded(bounded(k, s_ref, cap), jnp.max), jnp.maximum)
    return jnp.max(peak, axis=0, keepdims=True)


def exponentials(k, s_ref, cap, peak):
    return jnp.exp2((bounded(k, s_ref, cap) - peak) * SCALE2)


def head_rows(own, crossed, g, offset=0):
    at = slice(offset + g * HEAD, offset + (g + 1) * HEAD)
    return jnp.concatenate([own[:, at], crossed[:, at]], axis=0)


def put_rows(g, columns, own, crossed):
    rows = columns.T.astype(BF16)
    at = slice(g * HEAD, (g + 1) * HEAD)
    own[:, at] = rows[:ROWS]
    crossed[:, at] = rows[ROWS:]


def fwd_kernel(where_ref, q_ref, qx_ref, *refs):
    blocks, refs = refs[:SLOTS], refs[SLOTS + 1 :]
    blocks = blocks[:1] + blocks[4:] + blocks[1:4]
    o_own, o_cross, cap, s_ref, e_ref, keys, vt_ref = refs
    fill_cap(where_ref, blocks, cap)
    for k, b in enumerate(blocks):
        keys[slot(k), :] = b[:PAIR, :HEAD]
        vt_ref[:, slot(k)] = b[:PAIR, HEAD:].T

    def score(g):
        s_ref[g % 2] = dot(keys[...], head_rows(q_ref, qx_ref, g, 2 * HALF).T)

    score(0)
    for g in range(GROUP):
        now = g % 2
        if g + 1 < GROUP:
            score(g + 1)
        top = row_peak(s_ref.at[now], cap)
        total = None
        for k in range(SLOTS):
            expo = exponentials(k, s_ref.at[now], cap, top)
            e_ref[now, slot(k), :] = expo.astype(BF16)
            total = joined(total, folded(expo, jnp.sum), jnp.add)
        inv = 1.0 / jnp.sum(total, axis=0, keepdims=True)
        put_rows(g, dot(vt_ref[...], e_ref[now]) * inv, o_own, o_cross)


def bwd_kernel(where_ref, qd_ref, qdx_ref, *refs):
    blocks, refs = refs[:SLOTS], refs[SLOTS:]
    dq_own, dq_cross = refs[:2]
    parts, refs = refs[2 : SLOTS + 2], refs[SLOTS + 2 :]
    cap, s_ref, dp_ref, e_ref, ds_ref, qs_ref, gs_ref, acc, keys, values, kt_ref, turned = refs
    fill_cap(where_ref, blocks, cap)
    for k, b in enumerate(blocks):
        keys[slot(k), :] = b[:PAIR, :HEAD]
        values[slot(k), :] = b[:PAIR, HEAD:]
        kt_ref[:, slot(k)] = b[:PAIR, :HEAD].T

    def rows_of(which, g):
        return head_rows(qd_ref, qdx_ref, g, which * HALF)

    def products(g):
        for i, (block, out) in enumerate(((keys, s_ref), (values, dp_ref))):
            turned[g % 2, i] = rows_of(i, g).T
            out[g % 2] = dot(block[...], turned[g % 2, i])

    def span_of(g, count=1):
        return slice(g * PAIR, (g + count) * PAIR)

    def key_terms(g):
        span = span_of(g, 2)
        both = dot_nt(qs_ref[:, span], ds_ref[:, span]), dot_nt(gs_ref[:, span], e_ref[:, span])
        for i, terms in enumerate(both):
            acc[i] = terms if g == 0 else acc[i] + terms

    products(0)
    for g in range(GROUP):
        now = g % 2
        cols = span_of(g)
        if g + 1 < GROUP:
            products(g + 1)
        if g > 1 and g % 2 == 0:
            key_terms(g - 2)
        top = row_peak(s_ref.at[now], cap)
        total = inner = None
        for k in range(SLOTS):
            expo = exponentials(k, s_ref.at[now], cap, top)
            e_ref[slot(k), cols] = expo.astype(BF16)
            total = joined(total, folded(expo, jnp.sum), jnp.add)
            inner = joined(inner, folded(expo * dp_ref[now, slot(k), :], jnp.sum), jnp.add)
        inv = 1.0 / jnp.sum(total, axis=0, keepdims=True)
        delta = jnp.sum(inner, axis=0, keepdims=True) * inv
        qs_ref[:, cols] = (turned[now, 0].astype(F32) * inv).astype(BF16)
        gs_ref[:, cols] = (turned[now, 1].astype(F32) * inv).astype(BF16)
        for k in range(SLOTS):
            ds = (dp_ref[now, slot(k), :] - delta).astype(BF16)
            ds_ref[slot(k), cols] = e_ref[slot(k), cols] * ds
        put_rows(g, dot(kt_ref[...], ds_ref[:, cols]) * (inv * SCALE), dq_own, dq_cross)
    key_terms(GROUP - 2)
    for k in range(SLOTS):
        parts[k][:, :HEAD] = (acc[0, :, slot(k)] * SCALE).T.astype(BF16)
        parts[k][:, HEAD:] = acc[1, :, slot(k)].T.astype(BF16)


MATMUL = 2 * GROUP * PAIR * KEYS * HEAD
FINAL_FLOPS = 2 * MATMUL


def run_fwd(where, own, crossed, blocks, after):
    scratch = [
        pltpu.VMEM((KEYS, PAIR), F32),
        pltpu.VMEM((2, KEYS, PAIR), F32),
        pltpu.VMEM((2, KEYS, PAIR), BF16),
        pltpu.VMEM((KEYS, HEAD), BF16),
        pltpu.VMEM((HEAD, KEYS), BF16),
    ]
    return call(
        fwd_kernel,
        [shape(ROWS, HALF)] * 2,
        [VMEM] * (2 + SLOTS) + [ANY] * 1,
        scratch,
        2 * MATMUL,
        2**21,
        "fwd",
        limit=20,
    )(where, own, crossed, *blocks, *after)


def run_bwd(where, own, crossed, blocks):
    outs = [shape(ROWS, HALF)] * 2 + [shape(PAIR, 2 * HEAD)] * SLOTS
    scratch = [
        pltpu.VMEM((KEYS, PAIR), F32),
        pltpu.VMEM((2, KEYS, PAIR), F32),
        pltpu.VMEM((2, KEYS, PAIR), F32),
        pltpu.VMEM((KEYS, GROUP * PAIR), BF16),
        pltpu.VMEM((KEYS, GROUP * PAIR), BF16),
        pltpu.VMEM((HEAD, GROUP * PAIR), BF16),
        pltpu.VMEM((HEAD, GROUP * PAIR), BF16),
        pltpu.VMEM((2, HEAD, KEYS), F32),
        pltpu.VMEM((KEYS, HEAD), BF16),
        pltpu.VMEM((KEYS, HEAD), BF16),
        pltpu.VMEM((HEAD, KEYS), BF16),
        pltpu.VMEM((2, 2, HEAD, PAIR), BF16),
    ]
    out = call(
        bwd_kernel,
        outs,
        2 + SLOTS,
        scratch,
        5 * MATMUL,
        2**22,
        "bwd",
        limit=32,
    )(where, own, crossed, *blocks)
    return out[0], out[1], out[2:]


def along_z(block, distance):
    n = lax.axis_size("cp")
    return lax.ppermute(block, "cp", [(i, (i + 2 * distance) % n) for i in range(n)])


def swapped(block):
    return lax.ppermute(block, "cp", [(i, i ^ 1) for i in range(lax.axis_size("cp"))])


def handed(block, distance):
    n = lax.axis_size("section")
    return lax.ppermute(block, "section", [(i, (i + distance) % n) for i in range(n)])


def handed_across(block, distance):
    n, m = lax.axis_size("section"), lax.axis_size("cp")
    route = [
        (s * m + c, (s + distance) % n * m + (c ^ 1)) for s in range(n) for c in range(m)
    ]
    return lax.ppermute(block, ("section", "cp"), route)


def split(where, *arrays):
    scratch = [
        pltpu.VMEM((4, ROWS, 2 * HEAD), BF16),
        pltpu.VMEM((2, 1, ROWS), jnp.int32),
        pltpu.SemaphoreType.DMA((6,)),
    ]
    outs = [shape(ROWS + TAIL, 4 * HEAD)] * 2
    return call(split_kernel, outs, [HBM] * 6, scratch, name="split")(where, *arrays)


def join(where, keep, got, through):
    return pl.pallas_call(
        join_kernel,
        out_shape=[shape(PAIR + TAIL, 2 * HEAD)] * 2 + [shape(*through.shape)],
        in_specs=[SMEM] + [VMEM] * 2 + [ANY],
        out_specs=[VMEM] * 2 + [ANY],
        input_output_aliases={3: 2},
        compiler_params=pltpu.CompilerParams(vmem_limit_bytes=4 * 2**20),
        name="join",
    )(where, keep, got, through)


def tied_kernel(where_ref, held, after, out):
    del where_ref, held, after, out


def tied(where, held, after):
    return pl.pallas_call(
        tied_kernel,
        out_shape=shape(*held.shape),
        in_specs=[SMEM, ANY, ANY],
        out_specs=ANY,
        input_output_aliases={1: 0},
        compiler_params=pltpu.CompilerParams(vmem_limit_bytes=2**20),
        name="tied",
    )(where, held, after)


def per_device(qf, kf, vf, sf, qb, kb, vb, sb, grad):
    index = lax.axis_index("cp")
    side = index % 2
    where = jnp.stack([side, index // 2]).astype(jnp.int32)
    qf, kf, vf, qb, kb, vb, grad = (a[0] for a in (qf, kf, vf, qb, kb, vb, grad))
    qf, kf, vf, sf, qb, kb, vb, sb, grad = (
        pltpu.with_memory_space_constraint(a, pltpu.HBM)
        for a in (qf, kf, vf, sf, qb, kb, vb, sb, grad)
    )

    keep, send = split(where, kb, vb, sb, kf, vf, sf)
    own, halves = call(
        halves_kernel,
        [shape(ROWS, 3 * HALF)] * 2,
        [HBM] * 3 + [ANY],
        [pltpu.SemaphoreType.DMA((6,))],
        name="halves",
    )(where, qb, grad, qf, send)
    b0, f0, halves = join(where, keep, swapped(send), halves)
    b4 = along_z(b0, -2)
    b2 = along_z(b0, 2)
    b1 = along_z(b0, 1)
    crossed = swapped(halves)
    b4 = along_z(b4, -2)
    b3 = along_z(b2, 1)
    f0 = tied(where, f0, b2)
    f4, f3, f2, f1 = (along_z(f0, k) for k in (4, 3, 2, 1))
    blocks_f = (f0, f2, f3, f4, f1)

    dq_own, dq_cross, parts = run_bwd(where, own, crossed, (b0, b1, b2, b3, b4))
    far = along_z(parts[4], -1)
    three = (parts[3].astype(F32) + far.astype(F32)).astype(BF16)
    terms = [parts[0]] + [along_z(parts[k], -k) for k in (2, 1)] + [along_z(three, -3)]
    dq = handed(dq_own, -1), handed_across(dq_cross, -1)
    o_own, o_cross = run_fwd(where, own, crossed, blocks_f, (three,))
    dq = handed(dq_own, -1), handed_across(dq_cross, -1)
    (summed,) = call(
        total_kernel, [shape(PAIR, 2 * HEAD)], [VMEM] * 4 + [ANY] * 2, name="total"
    )(where, *terms, *dq)
    received = handed(summed, -1)
    attn_out, token = call(
        output_kernel,
        [shape(ROWS, 2 * HALF), shape(TAIL, HEAD)],
        2,
        [pltpu.SemaphoreType.DMA((2,))],
        FINAL_FLOPS,
        name="output",
        place=[HBM, VMEM],
    )(where, handed(o_own, 1), handed_across(o_cross, 1))
    grads = call(
        final_kernel,
        [shape(ROWS, 2 * HALF)] + [shape(ROWS, 2 * HEAD)] * 2,
        [VMEM] * 4 + [ANY],
        [pltpu.SemaphoreType.DMA((6,))],
        name="final",
        place=HBM,
    )(where, *dq, received, swapped(received[ROWS:]), token)
    return tuple(out[None] for out in (attn_out, *grads))


def solution(mesh):
    wide = P("section", "cp", "tp")
    flat = P("section", "cp")
    return jax.shard_map(
        per_device,
        mesh=mesh,
        in_specs=(wide, wide, wide, flat, wide, wide, wide, flat, wide),
        out_specs=(wide, wide, wide, wide),
        check_vma=False,
    )
```
